32 devices in a mesh: slot: 8 (over z, y), space: 4 (over x, core).
Axes of the slice: x: 2, y: 2, z: 4, core: 2. Of those that a mesh axis runs over, the one named last changes fastest.
Arguments:
- queries: bfloat16 [2048, 1024], P('space'), may hold values from -150 to 150
- raw_clip: bfloat16 [8, 8, 64, 2048], P(None, 'space', None, 'slot'), may hold values from -60 to 60
- pool_weight: bfloat16 [27, 2048], P(None, 'slot'), may hold values from -1.25 to 1.25
- old_memory: bfloat16 [8, 4, 4, 32, 2048], P('slot', None, 'space'), may hold values from -6 to 6
- valid_columns: int32 [9], replicated, may hold values from 16 to 32, as said below
- out_weight: bfloat16 [1024, 1024], replicated, may hold values from -0.1875 to 0.1875
Outputs:
- attended: bfloat16 [2048, 1024], P('space')
- fresh_memory: bfloat16 [4, 4, 32, 2048], P(None, 'space', None, 'slot')
- aged_memory: bfloat16 [8, 4, 4, 32, 2048], P('slot', None, 'space')
The draws below stay inside these ranges and needn't reach their ends.
Inputs may be any that keep to these rules, and one draw needn't show every extreme that they name: `valid_columns`: at least one entry equals 32.
All inputs are finite; a program needn't handle non-finite values.
Results may differ from the reference program's by a relative error of at most 0.0085.
Values may be sent and summed in bfloat16 or wider, within the bound.
No kernel may reach another device: no remote copies, remote signals or barrier semaphores. Data moves between devices by JAX's collectives and lax.ppermute only.
A program may use at most 128 MiB of HBM per device.

```python
import jax
import jax.numpy as jnp
from jax import lax

D = 1024
H = 16
HD = 64
QDEV = 512
MF = 4
MC = 32
MR = 4
CF = 8
RR = 8
CC = 64
MTOK = 512
QTOK = 2048
N_SLOT = 8


def draw_old_memory(key, part):
    shape_full = (N_SLOT, MF, MR, MC, 2 * D)
    sample = jax.random.normal(jax.random.fold_in(key, 101), shape_full, jnp.float32)
    return jnp.clip(sample, -6.0, 6.0).astype(jnp.bfloat16)


def draw_queries(key, part):
    sample = 2.5 * jax.random.normal(jax.random.fold_in(key, 111), (QTOK, D), jnp.float32)
    sample = jnp.clip(sample, -15.0, 15.0)
    return sample.astype(jnp.bfloat16)


def draw_raw_clip(key, part):
    shape_full = (CF, RR, CC, 2 * D)
    token_scale = jnp.exp(jax.random.uniform(jax.random.fold_in(key, 301), (CF, RR, CC, 1), jnp.float32, 0.0, jnp.log(10.0)))
    channel_scale = jnp.exp(jax.random.uniform(jax.random.fold_in(key, 302), (2 * D,), jnp.float32, jnp.log(0.1), 0.0))
    sample = jnp.clip(jax.random.normal(jax.random.fold_in(key, 303), shape_full, jnp.float32), -6.0, 6.0)
    return jnp.clip(sample * token_scale * channel_scale, -60.0, 60.0).astype(jnp.bfloat16)


def draw_valid_columns(key, part):
    counts = jax.random.randint(jax.random.fold_in(key, 401), (N_SLOT + 1,), MC // 2, MC + 1, jnp.int32)
    full_slot = jax.random.randint(jax.random.fold_in(key, 402), (), 0, N_SLOT + 1, jnp.int32)
    return counts.at[full_slot].set(MC)


def level_of(own_key, shape, split, least, top_value):
    loudness = 1.0
    for dim, parts in split:
        heights = jax.random.uniform(jax.random.fold_in(jax.random.fold_in(own_key, 6), dim), (parts,), jnp.float32, least / len(split), top_value / len(split))
        loudness = loudness * jnp.repeat(jnp.exp(heights), shape[dim] // parts).reshape((-1,) + (1,) * (len(shape) - 1 - dim))
    return loudness


def gaussian(stream_key, shape, width, bound, cuts=(), held_as=jnp.bfloat16):
    gain = level_of(stream_key, shape, cuts, -0.22, 0.18) if cuts else 1.0
    drawn = jax.random.normal(stream_key, shape, jnp.float32) * width * gain
    return jnp.minimum(jnp.maximum(drawn, -bound), bound).astype(held_as)


def setup_inputs(seed: int = 0) -> dict:
    splits = jax.random.split(jax.random.key(seed), 7)
    queries = draw_queries(jax.random.fold_in(splits[6], 71), 0)
    raw_clip = draw_raw_clip(jax.random.fold_in(splits[6], 71), 0)
    pool_weight = gaussian(splits[2], (27, 2 * D), 27 ** -0.5, 1.25, ((1, 8),))
    old_memory = draw_old_memory(jax.random.fold_in(splits[6], 71), 0)
    valid_columns = draw_valid_columns(jax.random.fold_in(splits[6], 71), 0)
    out_weight = gaussian(splits[5], (D, D), D ** -0.5, 0.1875)
    return dict(queries=queries, raw_clip=raw_clip, pool_weight=pool_weight, old_memory=old_memory, valid_columns=valid_columns, out_weight=out_weight)


def pool_clip(raw_clip, pool_weight):
    raw_values = raw_clip.astype(jnp.float32)
    padded = jnp.pad(raw_values, ((1, 0), (1, 0), (1, 0), (0, 0)))
    weight = pool_weight.astype(jnp.float32)
    pooled = jnp.zeros((MF, MR, MC, 2 * D), jnp.float32)
    for frame_tap in range(3):
        for row_tap in range(3):
            for column_tap in range(3):
                tapped = padded[frame_tap:frame_tap + 2 * MF:2, row_tap:row_tap + 2 * MR:2, column_tap:column_tap + 2 * MC:2]
                pooled = pooled + weight[9 * frame_tap + 3 * row_tap + column_tap] * tapped
    shaped = pooled.reshape(MF, MR, MC, H, 2, HD)
    center = lax.optimization_barrier(jnp.mean(shaped, axis=-1, keepdims=True))
    centered = shaped - center
    spread = lax.optimization_barrier(jnp.mean(centered * centered, axis=-1, keepdims=True))
    normed = centered * lax.rsqrt(spread + 1e-06)
    return normed.reshape(MF, MR, MC, 2 * D).astype(jnp.bfloat16)

def reference(queries, raw_clip, pool_weight, old_memory, valid_columns, out_weight):
    fresh_memory = pool_clip(raw_clip, pool_weight)
    memory = jnp.concatenate([fresh_memory.reshape(MTOK, H, 2, HD), old_memory.reshape(N_SLOT * MTOK, H, 2, HD)], axis=0)
    key_total = (N_SLOT + 1) * MTOK
    memory_heads = memory.transpose(1, 0, 2, 3)
    token_index = jnp.arange(key_total, dtype=jnp.int32)
    slot_index = (token_index // MTOK).astype(jnp.int32)
    column = token_index % MC
    usable = column < valid_columns[slot_index]
    query_heads = queries.reshape(QTOK, H, HD).transpose(1, 0, 2)

    def one_head(head_inputs):
        head_memory, head_queries = head_inputs
        key_rows = head_memory[:, 0, :]
        value_rows = head_memory[:, 1, :]

        def one_block(query_block):
            scores = jnp.dot(query_block, key_rows.T, preferred_element_type=jnp.float32) * HD ** (-0.5)
            scores = jnp.where(usable[None, :], scores, -1e+30)
            peak = lax.optimization_barrier(jnp.max(scores, axis=1, keepdims=True))
            weights = jnp.where(usable[None, :], jnp.exp(scores - peak), 0.0)
            weight_sum = lax.optimization_barrier(jnp.sum(weights, axis=1, keepdims=True))
            weighted = jnp.dot(weights.astype(jnp.bfloat16), value_rows, preferred_element_type=jnp.float32)
            return weighted / weight_sum
        blocks = lax.map(one_block, head_queries.reshape(QTOK // QDEV, QDEV, HD))
        return blocks.reshape(QTOK, HD)
    mixed_heads = lax.map(one_head, (memory_heads, query_heads))
    mixed = mixed_heads.transpose(1, 0, 2).reshape(QTOK, D).astype(jnp.bfloat16)
    attended = jnp.dot(mixed, out_weight, preferred_element_type=jnp.float32).astype(jnp.bfloat16)
    aged_memory = jnp.concatenate([jnp.zeros_like(old_memory[:1]), old_memory[:-1]], axis=0)
    return (attended, fresh_memory, aged_memory)
```

```python
from functools import partial

import jax
import jax.numpy as jnp
from jax import lax
from jax.experimental import pallas as pl
from jax.experimental.pallas import tpu as pltpu
from jax.sharding import PartitionSpec as P

H = 16
MASKED = -1e30
VMEM_LIMIT = 48 * 1024 * 1024
VMEM = pltpu.VMEM
SMEM = pltpu.SMEM


def params(**more):
    return pltpu.CompilerParams(vmem_limit_bytes=VMEM_LIMIT, **more)


def lanes_of(shape):
    return lax.broadcasted_iota(jnp.int32, shape, len(shape) - 1)


def exchange(block, axis, distance):
    size = lax.axis_size(axis)
    return lax.ppermute(block, axis, [(i, i ^ distance) for i in range(size)])


def from_behind(block, axis, distance):
    devices = range(lax.axis_size(axis))
    return lax.ppermute(block, axis, [(i - distance, i) for i in devices if i - distance in devices])


def pool_kernel(head_size, raw_ref, halo_ref, weight_ref, out_ref, slabs):
    frames, rows, columns, channels = raw_ref.shape
    frames_out, columns_out = frames // 2, columns // 2
    pieces, _, _, wide = slabs.shape
    group = lax.broadcasted_iota(jnp.int32, (wide, wide), 0) // head_size
    averaging = jnp.where(
        group == lanes_of((wide, wide)) // head_size, 1.0 / head_size, 0.0
    ).astype(jnp.float32)
    first_row = lax.broadcasted_iota(jnp.int32, (columns_out, wide), 0) == 0
    mean = partial(
        jnp.dot, precision=lax.Precision.HIGHEST, preferred_element_type=jnp.float32
    )
    for piece in range(pieces):
        lanes = slice(piece * wide, (piece + 1) * wide)
        for f in range(frames):
            slabs[piece, 3 * f] = halo_ref[f, 0, :, lanes].astype(jnp.float32)
            slabs[piece, 3 * f + 1] = raw_ref[f, 0, :, lanes].astype(jnp.float32)
            slabs[piece, 3 * f + 2] = raw_ref[f, 1, :, lanes].astype(jnp.float32)
        weight = weight_ref[:, lanes].astype(jnp.float32)
        for f in range(frames_out):
            sums = [jnp.zeros((columns_out, wide), jnp.float32) for _ in range(3)]
            for a in range(3):
                frame = 2 * f + a - 1
                if frame < 0:
                    continue
                for b in range(3):
                    even = slabs[piece, 3 * frame + b, pl.ds(0, columns_out, stride=2), :]
                    odd = slabs[piece, 3 * frame + b, pl.ds(1, columns_out, stride=2), :]
                    for g, tapped in enumerate((odd, even, odd)):
                        tap = 9 * a + 3 * b + g
                        sums[g] = sums[g] + weight[tap : tap + 1] * tapped
            behind = jnp.where(first_row, 0.0, pltpu.roll(sums[0], 1, 0))
            pooled = behind + sums[1] + sums[2]
            centered = pooled - mean(pooled, averaging)
            spread = mean(centered * centered, averaging)
            out_ref[f, 0, :, lanes] = (centered * lax.rsqrt(spread + 1e-06)).astype(jnp.bfloat16)


def pool(raw_clip, halo, pool_weight, head_size):
    frames, rows, columns, channels = raw_clip.shape
    return pl.pallas_call(
        partial(pool_kernel, head_size),
        out_shape=jax.ShapeDtypeStruct((frames // 2, 1, columns // 2, channels), jnp.bfloat16),
        in_specs=[pl.BlockSpec(memory_space=VMEM)] * 3,
        out_specs=pl.BlockSpec(memory_space=VMEM),
        scratch_shapes=[VMEM((channels // 128, 3 * frames, columns, 128), jnp.float32)],
        compiler_params=params(),
        name="pool",
    )(raw_clip, halo, pool_weight)


def cut_kernel(width, place_ref, memory_ref, *out_refs):
    place = place_ref[0]
    for distance, out_ref in enumerate(out_refs):
        start = pl.multiple_of((place ^ distance) * width, 128)
        out_ref[...] = memory_ref[:, pl.ds(start, width)]


def cut(place, memory, pieces):
    tokens, channels = memory.shape
    width = channels // pieces
    return pl.pallas_call(
        partial(cut_kernel, width),
        out_shape=[jax.ShapeDtypeStruct((tokens, width), memory.dtype)] * pieces,
        in_specs=[pl.BlockSpec(memory_space=SMEM), pl.BlockSpec(memory_space=VMEM)],
        out_specs=[pl.BlockSpec(memory_space=VMEM)] * pieces,
        compiler_params=params(),
        name="cut",
    )(place, memory)


def attend_kernel(
    head_size, columns, distances, final, has_state, place_ref, valid_ref, query_ref, *refs
):
    refs = list(refs)
    sources = [refs.pop(0), refs.pop(0)]
    state_ref = refs.pop(0) if has_state else None
    if final:
        value_ref, level_ref = refs.pop(0), refs.pop(0)
    else:
        state_out_ref = refs.pop(0)
    key_scratch, value_scratch = refs
    heads, key_count, wide = key_scratch.shape
    tokens = key_count // (2 * len(distances))

    @pl.when(pl.program_id(0) == 0)
    def _():
        lane = lanes_of((tokens, wide))
        column = lax.broadcasted_iota(jnp.int32, (tokens, wide), 0) % columns
        place = place_ref[0]
        for b, distance in enumerate(distances):
            valid = valid_ref[0] if distance is None else valid_ref[1 + (place ^ distance)]
            extra = jnp.where((lane == head_size) & (column >= valid), MASKED, 0.0)
            for c, source in enumerate(sources):
                row = (c * len(distances) + b) * tokens
                for h in range(heads):
                    tile = source[b * tokens : (b + 1) * tokens, h * wide : (h + 1) * wide]
                    tile = tile.astype(jnp.float32)
                    key_scratch[h, row : row + tokens] = jnp.where(
                        lane < head_size, tile, extra
                    ).astype(jnp.bfloat16)
                    value_scratch[h, row : row + tokens] = jnp.where(
                        lane < head_size, 1.0, tile
                    ).astype(jnp.bfloat16)

    block = query_ref.shape[0]
    lane = lanes_of((block, wide))
    queries = query_ref[...].astype(jnp.float32) * head_size ** (-0.5)
    values, levels = [], []
    for h in range(heads):
        rows = queries if h == 0 else pltpu.roll(queries, wide - h * head_size, 1)
        if rows.shape[1] < wide:
            rows = jnp.concatenate([rows, rows], axis=1)
        rows = jnp.where(lane < head_size, rows, jnp.where(lane == head_size, 1.0, 0.0))
        scores = lax.dot_general(
            rows.astype(jnp.bfloat16),
            key_scratch[h],
            (((1,), (1,)), ((), ())),
            preferred_element_type=jnp.float32,
        )
        peak = jnp.max(scores, axis=1, keepdims=True)
        if has_state:
            state = state_ref[h]
            old_peak = state[:, head_size // 2 : head_size // 2 + 1]
            peak = jnp.maximum(peak, old_peak)
        weights = jnp.exp(scores - peak).astype(jnp.bfloat16)
        total = jnp.dot(weights, value_scratch[h], preferred_element_type=jnp.float32)
        if has_state:
            total = total + state * jnp.exp(old_peak - peak)
        if final:
            weight_sum = total[:, :1]
            values.append(total[:, head_size:] / weight_sum)
            levels.append(jnp.broadcast_to(peak + jnp.log(weight_sum), (block, head_size)))
        else:
            keep = (lane >= head_size // 2) & (lane < head_size)
            state_out_ref[h] = jnp.where(keep, peak, total)
    if final:
        value_ref[...] = jnp.concatenate(values, axis=1).astype(value_ref.dtype)
        level = jnp.concatenate(levels, axis=1)
        if level.shape[1] < wide:
            level = jnp.concatenate([level, level], axis=1)
        turned = level.T
        for h in range(heads):
            level_ref[h : h + 1, :] = turned[h * head_size : h * head_size + 1, :]


def attend(
    place, valid, queries, sources, state, state_start, distances, columns, head_size, final, dtype
):
    rows, width = queries.shape
    heads = width // head_size
    wide = 2 * head_size
    key_count = 2 * sources[0].shape[0]
    block = min(256, rows)
    start = state_start // block
    whole = pl.BlockSpec(memory_space=VMEM)
    in_specs = [
        pl.BlockSpec(memory_space=SMEM),
        pl.BlockSpec(memory_space=SMEM),
        pl.BlockSpec((block, width), lambda i: (i, 0)),
        whole,
        whole,
    ]
    operands = [place, valid, queries, *sources]
    if state is not None:
        in_specs.append(pl.BlockSpec((heads, block, wide), lambda i: (0, i + start, 0)))
        operands.append(state)
    if final:
        out_shape = [
            jax.ShapeDtypeStruct((rows, width), dtype),
            jax.ShapeDtypeStruct((8, rows), jnp.float32),
        ]
        out_specs = [
            pl.BlockSpec((block, width), lambda i: (i, 0)),
            pl.BlockSpec((8, block), lambda i: (0, i)),
        ]
    else:
        out_shape = jax.ShapeDtypeStruct((heads, rows, wide), jnp.float32)
        out_specs = pl.BlockSpec((heads, block, wide), lambda i: (0, i, 0))
    return pl.pallas_call(
        partial(attend_kernel, head_size, columns, distances, final, state is not None),
        grid=(rows // block,),
        out_shape=out_shape,
        in_specs=in_specs,
        out_specs=out_specs,
        scratch_shapes=[VMEM((heads, key_count, wide), jnp.bfloat16)] * 2,
        compiler_params=params(),
        cost_estimate=pl.CostEstimate(
            flops=4 * rows * key_count * wide * heads,
            bytes_accessed=4 * key_count * wide * heads + 8 * rows * wide * heads,
            transcendentals=rows * key_count * heads,
        ),
        name="attend",
    )(*operands)


def merge_kernel(head_size, *refs):
    out_ref = refs[-1]
    refs = refs[:-1]
    values = [ref[...].astype(jnp.float32) for ref in refs[0::2]]
    rows, width = values[0].shape
    heads = width // head_size
    levels = []
    for ref in refs[1::2]:
        turned = jnp.concatenate(
            [jnp.broadcast_to(ref[h : h + 1, :], (head_size, rows)) for h in range(heads)], axis=0
        )
        levels.append(turned.T)
    top = levels[0]
    for level in levels[1:]:
        top = jnp.maximum(top, level)
    total = jnp.zeros((rows, width), jnp.float32)
    share = jnp.zeros((rows, width), jnp.float32)
    for value, level in zip(values, levels):
        factor = jnp.exp(level - top)
        total = total + value * factor
        share = share + factor
    out_ref[...] = (total / share).astype(out_ref.dtype)


def merge(parts, head_size):
    rows, width = parts[0][0].shape
    flat = [array for part in parts for array in part]
    return pl.pallas_call(
        partial(merge_kernel, head_size),
        out_shape=jax.ShapeDtypeStruct((rows, width), jnp.bfloat16),
        in_specs=[pl.BlockSpec(memory_space=VMEM)] * len(flat),
        out_specs=pl.BlockSpec(memory_space=VMEM),
        compiler_params=params(),
        name="merge",
    )(*flat)


def project_kernel(place_ref, weight_ref, *refs):
    out_ref = refs[-1]
    place = place_ref[0]
    total = None
    for distance, ref in enumerate(refs[:-1]):
        width = ref.shape[1]
        start = pl.multiple_of((place ^ distance) * width, width)
        term = jnp.dot(
            ref[...], weight_ref[pl.ds(start, width), :], preferred_element_type=jnp.float32
        )
        total = term if total is None else total + term
    out_ref[...] = total.astype(out_ref.dtype)


def project(place, out_weight, blocks):
    rows = blocks[0].shape[0]
    return pl.pallas_call(
        project_kernel,
        out_shape=jax.ShapeDtypeStruct((rows, out_weight.shape[1]), jnp.bfloat16),
        in_specs=[pl.BlockSpec(memory_space=SMEM)]
        + [pl.BlockSpec(memory_space=VMEM)] * (1 + len(blocks)),
        out_specs=pl.BlockSpec(memory_space=VMEM),
        compiler_params=params(),
        name="project",
    )(place, out_weight, *blocks)


def local(queries, raw_clip, pool_weight, old_memory, valid_columns, out_weight):
    query_rows, model_width = queries.shape
    head_size = model_width // H
    slots = lax.axis_size("slot")
    spaces = lax.axis_size("space")
    columns = old_memory.shape[3]
    width = model_width // slots
    slot_index = lax.axis_index("slot")
    place = slot_index.astype(jnp.int32).reshape(1)

    halo = from_behind(raw_clip[:, -1:], "space", 1)
    own_queries = lax.dynamic_slice_in_dim(queries, slot_index * width, width, axis=1)
    space_partners = range(2, spaces, 2)
    all_queries = [own_queries] + [exchange(own_queries, "space", d) for d in space_partners]

    resident = old_memory.reshape(-1, old_memory.shape[-1])
    pieces = cut(place, resident, slots)
    received = [pieces[0]] + [exchange(pieces[d], "slot", d) for d in range(1, slots)]

    fresh = pool(raw_clip, halo, pool_weight, head_size)
    fresh_rows = fresh.reshape(-1, fresh.shape[-1])

    half = slots // 2
    first = jnp.concatenate([fresh_rows] + received[:half], axis=0)
    first_other = exchange(first, "space", 1)
    second = jnp.concatenate(received[half:], axis=0)
    second_other = exchange(second, "space", 1)

    call = partial(attend, place, valid_columns, columns=columns, head_size=head_size)
    state = call(
        jnp.concatenate(all_queries, axis=0),
        (first, first_other),
        None,
        0,
        distances=(None,) + tuple(range(half)),
        final=False,
        dtype=None,
    )
    parts = []
    for k in list(range(1, len(all_queries))) + [0]:
        value, level = call(
            all_queries[k],
            (second, second_other),
            state,
            k * query_rows,
            distances=tuple(range(half, slots)),
            final=True,
            dtype=jnp.bfloat16 if k else jnp.float32,
        )
        if k:
            value = exchange(value, "space", 2 * k)
            level = exchange(level, "space", 2 * k)
        parts.append((value, level))
    mixed = merge(parts, head_size)

    blocks = {0: mixed}
    for d in range(2, slots, 2):
        blocks[d] = exchange(mixed, "slot", d)
    for d in range(0, slots, 2):
        blocks[d + 1] = exchange(blocks[d], "slot", 1)
    attended = project(place, out_weight, [blocks[d] for d in range(slots)])
    aged_memory = from_behind(old_memory, "slot", 1)
    return (attended, fresh, aged_memory)


def solution(mesh):
    return jax.shard_map(
        local,
        mesh=mesh,
        in_specs=(
            P("space", None),
            P(None, "space", None, "slot"),
            P(None, "slot"),
            P("slot", None, "space", None, None),
            P(),
            P(),
        ),
        out_specs=(
            P("space", None),
            P(None, "space", None, "slot"),
            P("slot", None, "space", None, None),
        ),
        check_vma=False,
    )
```

```python
from functools import partial

import jax
import jax.numpy as jnp
from jax import lax
from jax.experimental import pallas as pl
from jax.experimental.pallas import tpu as pltpu
from jax.sharding import PartitionSpec as P

H = 16
MASKED = -1e30
VMEM_LIMIT = 48 * 1024 * 1024
VMEM = pltpu.VMEM
SMEM = pltpu.SMEM


def params(**more):
    return pltpu.CompilerParams(vmem_limit_bytes=VMEM_LIMIT, **more)


def lanes_of(shape):
    return lax.broadcasted_iota(jnp.int32, shape, len(shape) - 1)


def exchange(block, axis, distance):
    size = lax.axis_size(axis)
    return lax.ppermute(block, axis, [(i, i ^ distance) for i in range(size)])


def from_behind(block, axis, distance):
    devices = range(lax.axis_size(axis))
    return lax.ppermute(block, axis, [(i - distance, i) for i in devices if i - distance in devices])


def pool_kernel(head_size, raw_ref, halo_ref, weight_ref, out_ref, slabs):
    frames, rows, columns, channels = raw_ref.shape
    frames_out, columns_out = frames // 2, columns // 2
    pieces, _, _, wide = slabs.shape
    group = lax.broadcasted_iota(jnp.int32, (wide, wide), 0) // head_size
    averaging = jnp.where(
        group == lanes_of((wide, wide)) // head_size, 1.0 / head_size, 0.0
    ).astype(jnp.float32)
    first_row = lax.broadcasted_iota(jnp.int32, (columns_out, wide), 0) == 0
    mean = partial(
        jnp.dot, precision=lax.Precision.HIGHEST, preferred_element_type=jnp.float32
    )
    for piece in range(pieces):
        lanes = slice(piece * wide, (piece + 1) * wide)
        for f in range(frames):
            slabs[piece, 3 * f] = halo_ref[f, rows - 1, :, lanes].astype(jnp.float32)
            slabs[piece, 3 * f + 1] = raw_ref[f, 0, :, lanes].astype(jnp.float32)
            slabs[piece, 3 * f + 2] = raw_ref[f, 1, :, lanes].astype(jnp.float32)
        weight = weight_ref[:, lanes].astype(jnp.float32)
        for f in range(frames_out):
            sums = [jnp.zeros((columns_out, wide), jnp.float32) for _ in range(3)]
            for a in range(3):
                frame = 2 * f + a - 1
                if frame < 0:
                    continue
                for b in range(3):
                    even = slabs[piece, 3 * frame + b, pl.ds(0, columns_out, stride=2), :]
                    odd = slabs[piece, 3 * frame + b, pl.ds(1, columns_out, stride=2), :]
                    for g, tapped in enumerate((odd, even, odd)):
                        tap = 9 * a + 3 * b + g
                        sums[g] = sums[g] + weight[tap : tap + 1] * tapped
            behind = jnp.where(first_row, 0.0, pltpu.roll(sums[0], 1, 0))
            pooled = behind + sums[1] + sums[2]
            centered = pooled - mean(pooled, averaging)
            spread = mean(centered * centered, averaging)
            out_ref[f, 0, :, lanes] = (centered * lax.rsqrt(spread + 1e-06)).astype(jnp.bfloat16)


def pool(raw_clip, halo, pool_weight, head_size):
    frames, rows, columns, channels = raw_clip.shape
    return pl.pallas_call(
        partial(pool_kernel, head_size),
        out_shape=jax.ShapeDtypeStruct((frames // 2, 1, columns // 2, channels), jnp.bfloat16),
        in_specs=[pl.BlockSpec(memory_space=VMEM)] * 3,
        out_specs=pl.BlockSpec(memory_space=VMEM),
        scratch_shapes=[VMEM((channels // 128, 3 * frames, columns, 128), jnp.float32)],
        compiler_params=params(),
        name="pool",
    )(raw_clip, halo, pool_weight)


def cut_kernel(width, place_ref, memory_ref, *out_refs):
    place = place_ref[0]
    for distance, out_ref in enumerate(out_refs):
        start = pl.multiple_of((place ^ distance) * width, 128)
        out_ref[...] = memory_ref[:, pl.ds(start, width)]


def cut(place, memory, pieces):
    tokens, channels = memory.shape
    width = channels // pieces
    return pl.pallas_call(
        partial(cut_kernel, width),
        out_shape=[jax.ShapeDtypeStruct((tokens, width), memory.dtype)] * pieces,
        in_specs=[pl.BlockSpec(memory_space=SMEM), pl.BlockSpec(memory_space=VMEM)],
        out_specs=[pl.BlockSpec(memory_space=VMEM)] * pieces,
        compiler_params=params(),
        name="cut",
    )(place, memory)


def attend_kernel(
    head_size, columns, distances, final, has_state, place_ref, valid_ref, query_ref, *refs
):
    refs = list(refs)
    sources = [refs.pop(0) for _ in distances]
    state_ref = refs.pop(0) if has_state else None
    rows, width = query_ref.shape
    heads = width // head_size
    wide = 2 * head_size
    place = place_ref[0]
    biases, tokens = [], 0
    for source, distance in zip(sources, distances):
        column = lanes_of((1, source.shape[0])) % columns
        valid = valid_ref[0] if distance is None else valid_ref[1 + (place ^ distance)]
        biases.append(jnp.where(column < valid, 0.0, MASKED))
        tokens += source.shape[0]
    bias = jnp.concatenate(biases, axis=1)
    lane = lanes_of((rows, wide))
    queries = query_ref[...].astype(jnp.float32) * head_size ** (-0.5)
    memory, scores = [], []
    for h in range(heads):
        own = queries if h == 0 else pltpu.roll(queries, width - h * head_size, 1)
        if own.shape[1] < wide:
            own = jnp.concatenate([own, own], axis=1)
        own = jnp.where(lane < head_size, own, 0.0).astype(jnp.bfloat16)
        memory.append(
            jnp.concatenate([source[:, h * wide : (h + 1) * wide] for source in sources], axis=0)
        )
        product = lax.dot_general(
            own, memory[h], (((1,), (1,)), ((), ())), preferred_element_type=jnp.float32
        )
        scores.append(product + bias)
    weights, peaks = [], []
    for h in range(heads):
        peak = jnp.max(scores[h], axis=1, keepdims=True)
        if has_state:
            peak = jnp.maximum(peak, state_ref[h, :, head_size // 2 : head_size // 2 + 1])
        peaks.append(peak)
        weights.append(jnp.exp(scores[h] - peak).astype(jnp.bfloat16))
    values, levels = [], []
    memory_lane = lanes_of((tokens, wide))
    for h in range(heads):
        ones_and_values = jnp.where(memory_lane < head_size, 1.0, memory[h].astype(jnp.float32))
        total = jnp.dot(
            weights[h], ones_and_values.astype(jnp.bfloat16), preferred_element_type=jnp.float32
        )
        if has_state:
            state = state_ref[h]
            old_peak = state[:, head_size // 2 : head_size // 2 + 1]
            total = total + state * jnp.exp(old_peak - peaks[h])
        if final:
            weight_sum = total[:, :1]
            values.append(total[:, head_size:] * (1.0 / weight_sum))
            level = peaks[h] + jnp.log(weight_sum)
            levels.append(jnp.broadcast_to(level, (rows, head_size)))
        else:
            keep = (lane >= head_size // 2) & (lane < head_size)
            refs[0][h] = jnp.where(keep, peaks[h], total)
    if final:
        refs[0][...] = jnp.concatenate(values, axis=1).astype(refs[0].dtype)
        write_levels(refs[1], jnp.concatenate(levels, axis=1), head_size)


def write_levels(level_ref, level, head_size):
    if level.shape[1] < 128:
        level = jnp.concatenate([level, level], axis=1)
    turned = level.T
    for h in range(H):
        if (h + 1) * head_size <= level.shape[1]:
            level_ref[h : h + 1, :] = turned[h * head_size : h * head_size + 1, :]


def attend(
    place, valid, queries, sources, state, state_start, distances, columns, head_size, final, dtype
):
    rows, width = queries.shape
    heads = width // head_size
    wide = 2 * head_size
    key_count = sum(source.shape[0] for source in sources)
    block = min(512, rows)
    start = state_start // block
    whole = pl.BlockSpec(memory_space=VMEM)
    in_specs = [
        pl.BlockSpec(memory_space=SMEM),
        pl.BlockSpec(memory_space=SMEM),
        pl.BlockSpec((block, width), lambda i: (i, 0)),
    ] + [whole] * len(sources)
    operands = [place, valid, queries, *sources]
    if state is not None:
        in_specs.append(pl.BlockSpec((heads, block, wide), lambda i: (0, i + start, 0)))
        operands.append(state)
    if final:
        out_shape = [
            jax.ShapeDtypeStruct((rows, width), dtype),
            jax.ShapeDtypeStruct((8, rows), jnp.float32),
        ]
        out_specs = [
            pl.BlockSpec((block, width), lambda i: (i, 0)),
            pl.BlockSpec((8, block), lambda i: (0, i)),
        ]
    else:
        out_shape = jax.ShapeDtypeStruct((heads, rows, wide), jnp.float32)
        out_specs = pl.BlockSpec((heads, block, wide), lambda i: (0, i, 0))
    return pl.pallas_call(
        partial(attend_kernel, head_size, columns, distances, final, state is not None),
        grid=(rows // block,),
        out_shape=out_shape,
        in_specs=in_specs,
        out_specs=out_specs,
        compiler_params=params(),
        cost_estimate=pl.CostEstimate(
            flops=4 * rows * key_count * wide * heads,
            bytes_accessed=4 * key_count * wide * heads + 8 * rows * wide * heads,
            transcendentals=rows * key_count * heads,
        ),
        name="attend",
    )(*operands)


def merge_kernel(head_size, count, final, *refs):
    parts, outs = refs[: 2 * count], refs[2 * count :]
    values = [ref[...].astype(jnp.float32) for ref in parts[0::2]]
    rows, width = values[0].shape
    heads = width // head_size
    levels = []
    for ref in parts[1::2]:
        spread = [jnp.broadcast_to(ref[h : h + 1, :], (head_size, rows)) for h in range(heads)]
        levels.append(jnp.concatenate(spread, axis=0).T)
    top = levels[0]
    for level in levels[1:]:
        top = jnp.maximum(top, level)
    total = jnp.zeros((rows, width), jnp.float32)
    share = jnp.zeros((rows, width), jnp.float32)
    for value, level in zip(values, levels):
        factor = jnp.exp(level - top)
        total = total + value * factor
        share = share + factor
    outs[0][...] = (total / share).astype(outs[0].dtype)
    if not final:
        write_levels(outs[1], top + jnp.log(share), head_size)


def merge(parts, rows, head_size, final):
    width = parts[0][0].shape[1]
    operands, in_specs = [], []
    for value, level, block in parts:
        operands += [value, level]
        in_specs += [
            pl.BlockSpec((rows, width), lambda i, block=block: (block, 0)),
            pl.BlockSpec((8, rows), lambda i, block=block: (0, block)),
        ]
    out_shape = [
        jax.ShapeDtypeStruct((rows, width), jnp.bfloat16),
        jax.ShapeDtypeStruct((8, rows), jnp.float32),
    ]
    out_specs = [
        pl.BlockSpec((rows, width), lambda i: (0, 0)),
        pl.BlockSpec((8, rows), lambda i: (0, 0)),
    ]
    keep = 1 if final else 2
    return pl.pallas_call(
        partial(merge_kernel, head_size, len(parts), final),
        grid=(1,),
        out_shape=out_shape[:keep],
        in_specs=in_specs,
        out_specs=out_specs[:keep],
        compiler_params=params(),
        name="merge",
    )(*operands)


def project_kernel(place_ref, weight_ref, *refs):
    out_ref = refs[-1]
    place = place_ref[0]
    total = None
    for distance, ref in enumerate(refs[:-1]):
        width = ref.shape[1]
        start = pl.multiple_of((place ^ distance) * width, width)
        term = jnp.dot(
            ref[...], weight_ref[pl.ds(start, width), :], preferred_element_type=jnp.float32
        )
        total = term if total is None else total + term
    out_ref[...] = total.astype(out_ref.dtype)


def project(place, out_weight, blocks):
    rows = blocks[0].shape[0]
    return pl.pallas_call(
        project_kernel,
        out_shape=jax.ShapeDtypeStruct((rows, out_weight.shape[1]), jnp.bfloat16),
        in_specs=[pl.BlockSpec(memory_space=SMEM)]
        + [pl.BlockSpec(memory_space=VMEM)] * (1 + len(blocks)),
        out_specs=pl.BlockSpec(memory_space=VMEM),
        compiler_params=params(),
        name="project",
    )(place, out_weight, *blocks)


def local(queries, raw_clip, pool_weight, old_memory, valid_columns, out_weight):
    query_rows, model_width = queries.shape
    head_size = model_width // H
    slots = lax.axis_size("slot")
    spaces = lax.axis_size("space")
    columns = old_memory.shape[3]
    width = model_width // slots
    slot_index = lax.axis_index("slot")
    place = slot_index.astype(jnp.int32).reshape(1)

    resident = old_memory.reshape(-1, old_memory.shape[-1])
    pieces = cut(place, resident, slots)
    received = {0: pieces[0]}
    for d in reversed(range(1, slots)):
        received[d] = exchange(pieces[d], "slot", d)

    own_queries = lax.dynamic_slice_in_dim(queries, slot_index * width, width, axis=1)
    evens = range(2, spaces, 2)
    near = jnp.concatenate([exchange(own_queries, "space", e) for e in evens] + [own_queries], 0)
    far = exchange(near, "space", 1)

    behind = from_behind(raw_clip, "space", 1)
    fresh = pool(raw_clip, behind, pool_weight, head_size)
    fresh_rows = fresh.reshape(-1, fresh.shape[-1])

    half = slots // 2
    first = (0,) + tuple(range(half, slots))
    second = tuple(range(1, half))
    call = partial(attend, place, valid_columns, columns=columns, head_size=head_size)
    state = call(
        jnp.concatenate([far, near], axis=0),
        [received[d] for d in first],
        None,
        0,
        distances=first,
        final=False,
        dtype=None,
    )
    sources = [fresh_rows] + [received[d] for d in second]
    call = partial(call, sources=sources, state=state, distances=(None,) + second, final=True)
    far_value, far_level = call(queries=far, state_start=0, dtype=jnp.bfloat16)
    core_value = exchange(far_value, "space", 1)
    core_level = exchange(far_level, "space", 1)
    parts = []
    for k, e in enumerate(evens):
        rows = slice(k * query_rows, (k + 1) * query_rows)
        value, level = call(
            queries=near[rows], state_start=far.shape[0] + k * query_rows, dtype=jnp.float32
        )
        value, level = merge(
            [(value, level, 0), (core_value, core_level, k)], query_rows, head_size, False
        )
        parts.append((exchange(value, "space", e), exchange(level, "space", e), 0))
    last = len(evens)
    value, level = call(
        queries=own_queries, state_start=far.shape[0] + last * query_rows, dtype=jnp.float32
    )
    parts = [(value, level, 0), (core_value, core_level, last)] + parts
    (mixed,) = merge(parts, query_rows, head_size, True)

    blocks = {0: mixed}
    for d in reversed(range(2, slots, 2)):
        blocks[d] = exchange(mixed, "slot", d)
    for d in range(0, slots, 2):
        blocks[d + 1] = exchange(blocks[d], "slot", 1)
    attended = project(place, out_weight, [blocks[d] for d in range(slots)])
    aged_memory = from_behind(old_memory, "slot", 1)
    return (attended, fresh, aged_memory)


def solution(mesh):
    return jax.shard_map(
        local,
        mesh=mesh,
        in_specs=(
            P("space", None),
            P(None, "space", None, "slot"),
            P(None, "slot"),
            P("slot", None, "space", None, None),
            P(),
            P(),
        ),
        out_specs=(
            P("space", None),
            P(None, "space", None, "slot"),
            P("slot", None, "space", None, None),
        ),
        check_vma=False,
    )
```

```python
from functools import partial

import jax
import jax.numpy as jnp
from jax import lax
from jax.experimental import pallas as pl
from jax.experimental.pallas import tpu as pltpu
from jax.sharding import PartitionSpec as P

H = 16
MASKED = -1e30
VMEM_LIMIT = 48 * 1024 * 1024
VMEM = pltpu.VMEM
SMEM = pltpu.SMEM


def params(**more):
    return pltpu.CompilerParams(vmem_limit_bytes=VMEM_LIMIT, **more)


def lanes_of(shape):
    return lax.broadcasted_iota(jnp.int32, shape, len(shape) - 1)


def exchange(block, axis, distance):
    size = lax.axis_size(axis)
    return lax.ppermute(block, axis, [(i, i ^ distance) for i in range(size)])


def from_behind(block, axis, distance):
    devices = range(lax.axis_size(axis))
    return lax.ppermute(block, axis, [(i - distance, i) for i in devices if i - distance in devices])


def pool_kernel(head_size, raw_ref, halo_ref, weight_ref, out_ref, slabs):
    frames, rows, columns, channels = raw_ref.shape
    frames_out, columns_out = frames // 2, columns // 2
    pieces, _, _, wide = slabs.shape
    group = lax.broadcasted_iota(jnp.int32, (wide, wide), 0) // head_size
    averaging = jnp.where(
        group == lanes_of((wide, wide)) // head_size, 1.0 / head_size, 0.0
    ).astype(jnp.float32)
    first_row = lax.broadcasted_iota(jnp.int32, (columns_out, wide), 0) == 0
    mean = partial(
        jnp.dot, precision=lax.Precision.HIGHEST, preferred_element_type=jnp.float32
    )
    for piece in range(pieces):
        lanes = slice(piece * wide, (piece + 1) * wide)
        for f in range(frames):
            slabs[piece, 3 * f] = halo_ref[f, rows - 1, :, lanes].astype(jnp.float32)
            slabs[piece, 3 * f + 1] = raw_ref[f, 0, :, lanes].astype(jnp.float32)
            slabs[piece, 3 * f + 2] = raw_ref[f, 1, :, lanes].astype(jnp.float32)
        weight = weight_ref[:, lanes].astype(jnp.float32)
        for f in range(frames_out):
            sums = [jnp.zeros((columns_out, wide), jnp.float32) for _ in range(3)]
            for a in range(3):
                frame = 2 * f + a - 1
                if frame < 0:
                    continue
                for b in range(3):
                    even = slabs[piece, 3 * frame + b, pl.ds(0, columns_out, stride=2), :]
                    odd = slabs[piece, 3 * frame + b, pl.ds(1, columns_out, stride=2), :]
                    for g, tapped in enumerate((odd, even, odd)):
                        tap = 9 * a + 3 * b + g
                        sums[g] = sums[g] + weight[tap : tap + 1] * tapped
            behind = jnp.where(first_row, 0.0, pltpu.roll(sums[0], 1, 0))
            pooled = behind + sums[1] + sums[2]
            centered = pooled - mean(pooled, averaging)
            spread = mean(centered * centered, averaging)
            out_ref[f, 0, :, lanes] = (centered * lax.rsqrt(spread + 1e-06)).astype(jnp.bfloat16)


def pool(raw_clip, halo, pool_weight, head_size):
    frames, rows, columns, channels = raw_clip.shape
    return pl.pallas_call(
        partial(pool_kernel, head_size),
        out_shape=jax.ShapeDtypeStruct((frames // 2, 1, columns // 2, channels), jnp.bfloat16),
        in_specs=[pl.BlockSpec(memory_space=VMEM)] * 3,
        out_specs=pl.BlockSpec(memory_space=VMEM),
        scratch_shapes=[VMEM((channels // 128, 3 * frames, columns, 128), jnp.float32)],
        compiler_params=params(),
        name="pool",
    )(raw_clip, halo, pool_weight)


def cut_kernel(width, place_ref, memory_ref, raw_ref, weight_ref, raw_out, weight_out, *out_refs):
    place = place_ref[0]
    for distance, out_ref in enumerate(out_refs):
        start = pl.multiple_of((place ^ distance) * width, 128)
        out_ref[...] = memory_ref[:, pl.ds(start, width)]
    raw_out[...] = raw_ref[...]
    weight_out[...] = weight_ref[...]


def cut(place, memory, raw_clip, pool_weight, pieces):
    tokens, channels = memory.shape
    width = channels // pieces
    out = [raw_clip, pool_weight]
    out += [jax.ShapeDtypeStruct((tokens, width), memory.dtype)] * pieces
    return pl.pallas_call(
        partial(cut_kernel, width),
        out_shape=[jax.ShapeDtypeStruct(o.shape, o.dtype) for o in out],
        in_specs=[pl.BlockSpec(memory_space=SMEM)] + [pl.BlockSpec(memory_space=VMEM)] * 3,
        out_specs=[pl.BlockSpec(memory_space=VMEM)] * len(out),
        compiler_params=params(),
        name="cut",
    )(place, memory, raw_clip, pool_weight)


def attend_kernel(head_size, columns, distances, place_ref, valid_ref, query_ref, *refs):
    sources, (value_ref, level_ref) = refs[: len(distances)], refs[len(distances) :]
    rows, width = query_ref.shape
    heads = width // head_size
    wide = 2 * head_size
    place = place_ref[0]
    biases = []
    for source, distance in zip(sources, distances):
        column = lanes_of((1, source.shape[0])) % columns
        valid = valid_ref[0] if distance is None else valid_ref[1 + (place ^ distance)]
        biases.append(jnp.where(column < valid, 0.0, MASKED))
    bias = jnp.concatenate(biases, axis=1)
    lane = lanes_of((rows, wide))
    queries = query_ref[...].astype(jnp.float32) * head_size ** (-0.5)
    memory, scores = [], []
    for h in range(heads):
        own = queries if h == 0 else pltpu.roll(queries, width - h * head_size, 1)
        if own.shape[1] < wide:
            own = jnp.concatenate([own, own], axis=1)
        own = jnp.where(lane < head_size, own, 0.0).astype(jnp.bfloat16)
        memory.append(
            jnp.concatenate([source[:, h * wide : (h + 1) * wide] for source in sources], axis=0)
        )
        product = lax.dot_general(
            own, memory[h], (((1,), (1,)), ((), ())), preferred_element_type=jnp.float32
        )
        scores.append(product + bias)
    weights, peaks = [], []
    for h in range(heads):
        peaks.append(jnp.max(scores[h], axis=1, keepdims=True))
        weights.append(jnp.exp(scores[h] - peaks[h]).astype(jnp.bfloat16))
    values, levels = [], []
    memory_lane = lanes_of(memory[0].shape)
    for h in range(heads):
        ones_and_values = jnp.where(memory_lane < head_size, 1.0, memory[h].astype(jnp.float32))
        total = jnp.dot(
            weights[h], ones_and_values.astype(jnp.bfloat16), preferred_element_type=jnp.float32
        )
        turned = pltpu.roll(total, head_size, 1)
        if h % 2:
            values.append(total / turned)
            levels.append(jnp.log(turned) + peaks[h])
        else:
            values.append(turned / total)
            levels.append(jnp.log(total) + peaks[h])
    if heads == 1:
        value_ref[...] = values[0][:, :head_size].astype(value_ref.dtype)
        level = levels[0]
    else:
        value_ref[...] = jnp.where(lane < head_size, *values).astype(value_ref.dtype)
        level = jnp.where(lane < head_size, *levels)
    write_levels(level_ref, level, heads, head_size)


def write_levels(level_ref, level, heads, head_size):
    turned = level.T
    for h in range(heads):
        level_ref[h : h + 1, :] = turned[h * head_size : h * head_size + 1, :]


def attend(place, valid, queries, sources, distances, columns, head_size, dtype):
    rows, width = queries.shape
    heads = width // head_size
    wide = 2 * head_size
    key_count = sum(source.shape[0] for source in sources)
    block = min(512, rows)
    return pl.pallas_call(
        partial(attend_kernel, head_size, columns, distances),
        grid=(rows // block,),
        out_shape=[
            jax.ShapeDtypeStruct((rows, width), dtype),
            jax.ShapeDtypeStruct((8, rows), jnp.float32),
        ],
        in_specs=[
            pl.BlockSpec(memory_space=SMEM),
            pl.BlockSpec(memory_space=SMEM),
            pl.BlockSpec((block, width), lambda i: (i, 0)),
        ]
        + [pl.BlockSpec(memory_space=VMEM)] * len(sources),
        out_specs=[
            pl.BlockSpec((block, width), lambda i: (i, 0)),
            pl.BlockSpec((8, block), lambda i: (0, i)),
        ],
        compiler_params=params(),
        cost_estimate=pl.CostEstimate(
            flops=4 * rows * key_count * wide * heads,
            bytes_accessed=4 * key_count * wide * heads + 8 * rows * wide * heads,
            transcendentals=rows * key_count * heads,
        ),
        name="attend",
    )(place, valid, queries, *sources)


def merge_kernel(head_size, count, final, *refs):
    parts, outs = refs[: 2 * count], refs[2 * count :]
    values = [ref[...].astype(jnp.float32) for ref in parts[0::2]]
    rows, width = values[0].shape
    heads = width // head_size
    levels = []
    for ref in parts[1::2]:
        spread = [jnp.broadcast_to(ref[h : h + 1, :], (head_size, rows)) for h in range(heads)]
        levels.append(jnp.concatenate(spread, axis=0).T)
    top = levels[0]
    for level in levels[1:]:
        top = jnp.maximum(top, level)
    total = jnp.zeros((rows, width), jnp.float32)
    share = jnp.zeros((rows, width), jnp.float32)
    for value, level in zip(values, levels):
        factor = jnp.exp(level - top)
        total = total + value * factor
        share = share + factor
    outs[0][...] = (total / share).astype(outs[0].dtype)
    if not final:
        level = top + jnp.log(share)
        if width < 128:
            level = jnp.concatenate([level, level], axis=1)
        write_levels(outs[1], level, heads, head_size)


def merge(parts, rows, head_size, final):
    width = parts[0][0].shape[1]
    operands, in_specs = [], []
    for value, level, block in parts:
        operands += [value, level]
        in_specs += [
            pl.BlockSpec((rows, width), lambda i, block=block: (block, 0)),
            pl.BlockSpec((8, rows), lambda i, block=block: (0, block)),
        ]
    out_shape = [
        jax.ShapeDtypeStruct((rows, width), jnp.bfloat16),
        jax.ShapeDtypeStruct((8, rows), jnp.float32),
    ]
    out_specs = [
        pl.BlockSpec((rows, width), lambda i: (0, 0)),
        pl.BlockSpec((8, rows), lambda i: (0, 0)),
    ]
    keep = 1 if final else 2
    return pl.pallas_call(
        partial(merge_kernel, head_size, len(parts), final),
        grid=(1,),
        out_shape=out_shape[:keep],
        in_specs=in_specs,
        out_specs=out_specs[:keep],
        compiler_params=params(),
        name="merge",
    )(*operands)


def project_kernel(distances, has_total, aged, place_ref, weight_ref, *refs):
    refs = list(refs)
    blocks = [refs.pop(0) for _ in distances]
    total_ref = refs.pop(0) if has_total else None
    if aged:
        aged_ref, out_ref, aged_out, semaphore = refs
        copy = pltpu.make_async_copy(aged_ref, aged_out, semaphore)
        copy.start()
    else:
        (out_ref,) = refs
    place = place_ref[0]
    width = blocks[0].shape[1]
    weights = []
    for distance in distances:
        start = pl.multiple_of((place ^ distance) * width, width)
        weights.append(weight_ref[pl.ds(start, width), :])
    total = jnp.dot(
        jnp.concatenate([block[...] for block in blocks], axis=1),
        jnp.concatenate(weights, axis=0),
        preferred_element_type=jnp.float32,
    )
    if has_total:
        total = total + total_ref[...]
    out_ref[...] = total.astype(out_ref.dtype)
    if aged:
        copy.wait()


def project(place, out_weight, blocks, distances, total=None, aged=None):
    rows, columns = blocks[0].shape[0], out_weight.shape[1]
    operands = [place, out_weight, *blocks]
    in_specs = [pl.BlockSpec(memory_space=SMEM)]
    in_specs += [pl.BlockSpec(memory_space=VMEM)] * (1 + len(blocks))
    dtype = jnp.float32 if total is None else jnp.bfloat16
    out_shape = [jax.ShapeDtypeStruct((rows, columns), dtype)]
    out_specs = [pl.BlockSpec(memory_space=VMEM)]
    scratch = []
    if total is not None:
        operands.append(total)
        in_specs.append(pl.BlockSpec(memory_space=VMEM))
    if aged is not None:
        operands.append(aged)
        in_specs.append(pl.BlockSpec(memory_space=pl.ANY))
        out_shape.append(jax.ShapeDtypeStruct(aged.shape, aged.dtype))
        out_specs.append(pl.BlockSpec(memory_space=pl.ANY))
        scratch.append(pltpu.SemaphoreType.DMA)
    return pl.pallas_call(
        partial(project_kernel, distances, total is not None, aged is not None),
        out_shape=out_shape,
        in_specs=in_specs,
        out_specs=out_specs,
        scratch_shapes=scratch,
        compiler_params=params(),
        cost_estimate=pl.CostEstimate(
            flops=2 * rows * columns * blocks[0].shape[1] * len(blocks),
            bytes_accessed=4 * rows * columns,
            transcendentals=0,
        ),
        name="project",
    )(*operands)


def after(array, *others):
    return lax.optimization_barrier((array, *others))[0]


def local(queries, raw_clip, pool_weight, old_memory, valid_columns, out_weight):
    query_rows, model_width = queries.shape
    head_size = model_width // H
    slots = lax.axis_size("slot")
    spaces = lax.axis_size("space")
    columns = old_memory.shape[3]
    width = model_width // slots
    slot_index = lax.axis_index("slot")
    place = slot_index.astype(jnp.int32).reshape(1)

    own_queries = lax.dynamic_slice_in_dim(queries, slot_index * width, width, axis=1)
    evens = range(2, spaces, 2)
    near = jnp.concatenate([exchange(own_queries, "space", e) for e in evens] + [own_queries], 0)

    resident = old_memory.reshape(-1, old_memory.shape[-1])
    raw_clip, pool_weight, *pieces = cut(place, resident, raw_clip, pool_weight, slots)
    received = {0: pieces[0]}
    for d in reversed(range(1, slots)):
        received[d] = exchange(pieces[d], "slot", d)

    far = exchange(after(near, received[slots - 1]), "space", 1)
    behind = from_behind(after(raw_clip, received[slots - 1]), "space", 1)
    fresh = pool(raw_clip, behind, pool_weight, head_size)
    fresh_rows = fresh.reshape(-1, fresh.shape[-1])
    aged_memory = from_behind(after(old_memory, *received.values()), "slot", 1)

    distances = tuple(range(slots))
    call = partial(
        attend,
        place,
        valid_columns,
        sources=[fresh_rows] + [received[d] for d in distances],
        distances=(None,) + distances,
        columns=columns,
        head_size=head_size,
    )
    far_value, far_level = call(queries=far, dtype=jnp.bfloat16)
    core_value = exchange(far_value, "space", 1)
    core_level = exchange(far_level, "space", 1)
    parts = []
    for k, e in enumerate(evens):
        rows = slice(k * query_rows, (k + 1) * query_rows)
        value, level = call(queries=near[rows], dtype=jnp.float32)
        value, level = merge(
            [(value, level, 0), (core_value, core_level, k)], query_rows, head_size, False
        )
        parts.append((exchange(value, "space", e), exchange(level, "space", e), 0))
    value, level = call(queries=own_queries, dtype=jnp.float32)
    parts = [(value, level, 0), (core_value, core_level, len(evens))] + parts
    (mixed,) = merge(parts, query_rows, head_size, True)

    blocks = {0: mixed}
    for d in reversed(range(2, slots, 2)):
        blocks[d] = exchange(mixed, "slot", d)
    for d in range(0, slots, 2):
        blocks[d + 1] = exchange(blocks[d], "slot", 1)
    half = slots // 2
    first, second = distances[:half], distances[half:]
    (total,) = project(place, out_weight, [blocks[d] for d in first], first)
    attended, aged_memory = project(
        place, out_weight, [blocks[d] for d in second], second, total, aged_memory
    )
    return (attended, fresh, aged_memory)


def solution(mesh):
    return jax.shard_map(
        local,
        mesh=mesh,
        in_specs=(
            P("space", None),
            P(None, "space", None, "slot"),
            P(None, "slot"),
            P("slot", None, "space", None, None),
            P(),
            P(),
        ),
        out_specs=(
            P("space", None),
            P(None, "space", None, "slot"),
            P("slot", None, "space", None, None),
        ),
        check_vma=False,
    )
```

```python
from functools import partial

import jax
import jax.numpy as jnp
from jax import lax
from jax.experimental import pallas as pl
from jax.experimental.pallas import tpu as pltpu
from jax.sharding import PartitionSpec as P

H = 16
MASKED = -1e30
VMEM_LIMIT = 48 * 1024 * 1024
VMEM = pltpu.VMEM
SMEM = pltpu.SMEM


def params(**more):
    return pltpu.CompilerParams(vmem_limit_bytes=VMEM_LIMIT, **more)


def lanes_of(shape):
    return lax.broadcasted_iota(jnp.int32, shape, len(shape) - 1)


def exchange(block, axis, distance):
    size = lax.axis_size(axis)
    return lax.ppermute(block, axis, [(i, i ^ distance) for i in range(size)])


def from_behind(block, axis, distance):
    devices = range(lax.axis_size(axis))
    return lax.ppermute(block, axis, [(i - distance, i) for i in devices if i - distance in devices])


def pool_kernel(head_size, raw_ref, halo_ref, weight_ref, out_ref, slabs):
    frames, rows, columns, channels = raw_ref.shape
    frames_out, columns_out = frames // 2, columns // 2
    pieces, _, _, wide = slabs.shape
    group = lax.broadcasted_iota(jnp.int32, (wide, wide), 0) // head_size
    averaging = jnp.where(
        group == lanes_of((wide, wide)) // head_size, 1.0 / head_size, 0.0
    ).astype(jnp.float32)
    first_row = lax.broadcasted_iota(jnp.int32, (columns_out, wide), 0) == 0
    mean = partial(
        jnp.dot, precision=lax.Precision.HIGHEST, preferred_element_type=jnp.float32
    )
    for piece in range(pieces):
        lanes = slice(piece * wide, (piece + 1) * wide)
        for f in range(frames):
            slabs[piece, 3 * f] = halo_ref[f, rows - 1, :, lanes].astype(jnp.float32)
            slabs[piece, 3 * f + 1] = raw_ref[f, 0, :, lanes].astype(jnp.float32)
            slabs[piece, 3 * f + 2] = raw_ref[f, 1, :, lanes].astype(jnp.float32)
        weight = weight_ref[:, lanes].astype(jnp.float32)
        for f in range(frames_out):
            sums = [jnp.zeros((columns_out, wide), jnp.float32) for _ in range(3)]
            for a in range(3):
                frame = 2 * f + a - 1
                if frame < 0:
                    continue
                for b in range(3):
                    even = slabs[piece, 3 * frame + b, pl.ds(0, columns_out, stride=2), :]
                    odd = slabs[piece, 3 * frame + b, pl.ds(1, columns_out, stride=2), :]
                    for g, tapped in enumerate((odd, even, odd)):
                        tap = 9 * a + 3 * b + g
                        sums[g] = sums[g] + weight[tap : tap + 1] * tapped
            behind = jnp.where(first_row, 0.0, pltpu.roll(sums[0], 1, 0))
            pooled = behind + sums[1] + sums[2]
            centered = pooled - mean(pooled, averaging)
            spread = mean(centered * centered, averaging)
            out_ref[f, 0, :, lanes] = (centered * lax.rsqrt(spread + 1e-06)).astype(jnp.bfloat16)


def pool(raw_clip, halo, pool_weight, head_size):
    frames, rows, columns, channels = raw_clip.shape
    return pl.pallas_call(
        partial(pool_kernel, head_size),
        out_shape=jax.ShapeDtypeStruct((frames // 2, 1, columns // 2, channels), jnp.bfloat16),
        in_specs=[pl.BlockSpec(memory_space=VMEM)] * 3,
        out_specs=pl.BlockSpec(memory_space=VMEM),
        scratch_shapes=[VMEM((channels // 128, 3 * frames, columns, 128), jnp.float32)],
        compiler_params=params(),
        name="pool",
    )(raw_clip, halo, pool_weight)


def cut_kernel(width, groups, place_ref, memory_ref, *out_refs):
    place = place_ref[0]
    tokens = memory_ref.shape[0]
    for group, out_ref in zip(groups, out_refs):
        for k, distance in enumerate(group):
            start = pl.multiple_of((place ^ distance) * width, 128)
            out_ref[k * tokens : (k + 1) * tokens] = memory_ref[:, pl.ds(start, width)]


def cut(place, memory, pieces, groups):
    tokens, channels = memory.shape
    width = channels // pieces
    return pl.pallas_call(
        partial(cut_kernel, width, groups),
        out_shape=[jax.ShapeDtypeStruct((len(g) * tokens, width), memory.dtype) for g in groups],
        in_specs=[pl.BlockSpec(memory_space=SMEM), pl.BlockSpec(memory_space=VMEM)],
        out_specs=[pl.BlockSpec(memory_space=VMEM)] * len(groups),
        compiler_params=params(),
        name="cut",
    )(place, memory)


def attend_kernel(
    head_size, columns, tokens, distances, place_ref, valid_ref, query_ref, *refs
):
    sources, (value_ref, level_ref) = refs[:-2], refs[-2:]
    rows, width = query_ref.shape
    heads = width // head_size
    wide = 2 * head_size
    place = place_ref[0]
    biases = []
    column = lanes_of((1, tokens)) % columns
    for distance in distances:
        valid = valid_ref[0] if distance is None else valid_ref[1 + (place ^ distance)]
        biases.append(jnp.where(column < valid, 0.0, MASKED))
    bias = jnp.concatenate(biases, axis=1)
    lane = lanes_of((rows, wide))
    queries = query_ref[...].astype(jnp.float32) * head_size ** (-0.5)
    memory, scores = [], []
    for h in range(heads):
        own = queries if h == 0 else pltpu.roll(queries, width - h * head_size, 1)
        if own.shape[1] < wide:
            own = jnp.concatenate([own, own], axis=1)
        own = jnp.where(lane < head_size, own, 0.0).astype(jnp.bfloat16)
        memory.append(
            jnp.concatenate([source[:, h * wide : (h + 1) * wide] for source in sources], axis=0)
        )
        product = lax.dot_general(
            own, memory[h], (((1,), (1,)), ((), ())), preferred_element_type=jnp.float32
        )
        scores.append(product + bias)
    weights, peaks = [], []
    for h in range(heads):
        peaks.append(jnp.max(scores[h], axis=1, keepdims=True))
        weights.append(jnp.exp(scores[h] - peaks[h]).astype(jnp.bfloat16))
    values, levels = [], []
    memory_lane = lanes_of(memory[0].shape)
    for h in range(heads):
        ones_and_values = jnp.where(memory_lane < head_size, 1.0, memory[h].astype(jnp.float32))
        total = jnp.dot(
            weights[h], ones_and_values.astype(jnp.bfloat16), preferred_element_type=jnp.float32
        )
        turned = pltpu.roll(total, head_size, 1)
        if h % 2:
            values.append(total / turned)
            levels.append(jnp.log(turned) + peaks[h])
        else:
            values.append(turned / total)
            levels.append(jnp.log(total) + peaks[h])
    if heads == 1:
        value_ref[...] = values[0][:, :head_size].astype(value_ref.dtype)
        level = levels[0]
    else:
        value_ref[...] = jnp.where(lane < head_size, *values).astype(value_ref.dtype)
        level = jnp.where(lane < head_size, *levels)
    write_levels(level_ref, level, heads, head_size)


def write_levels(level_ref, level, heads, head_size):
    turned = level.T
    for h in range(heads):
        level_ref[h : h + 1, :] = turned[h * head_size : h * head_size + 1, :]


def attend(place, valid, queries, sources, tokens, distances, columns, head_size, dtype):
    rows, width = queries.shape
    heads = width // head_size
    wide = 2 * head_size
    key_count = sum(source.shape[0] for source in sources)
    block = min(512, rows)
    return pl.pallas_call(
        partial(attend_kernel, head_size, columns, tokens, distances),
        grid=(rows // block,),
        out_shape=[
            jax.ShapeDtypeStruct((rows, width), dtype),
            jax.ShapeDtypeStruct((8, rows), jnp.float32),
        ],
        in_specs=[
            pl.BlockSpec(memory_space=SMEM),
            pl.BlockSpec(memory_space=SMEM),
            pl.BlockSpec((block, width), lambda i: (i, 0)),
        ]
        + [pl.BlockSpec(memory_space=VMEM)] * len(sources),
        out_specs=[
            pl.BlockSpec((block, width), lambda i: (i, 0)),
            pl.BlockSpec((8, block), lambda i: (0, i)),
        ],
        compiler_params=params(),
        cost_estimate=pl.CostEstimate(
            flops=4 * rows * key_count * wide * heads,
            bytes_accessed=4 * key_count * wide * heads + 8 * rows * wide * heads,
            transcendentals=rows * key_count * heads,
        ),
        name="attend",
    )(place, valid, queries, *sources)


def merge_kernel(head_size, count, final, *refs):
    parts, outs = refs[: 2 * count], refs[2 * count :]
    values = [ref[...].astype(jnp.float32) for ref in parts[0::2]]
    rows, width = values[0].shape
    heads = width // head_size
    levels = []
    for ref in parts[1::2]:
        spread = [jnp.broadcast_to(ref[h : h + 1, :], (head_size, rows)) for h in range(heads)]
        levels.append(jnp.concatenate(spread, axis=0).T)
    top = levels[0]
    for level in levels[1:]:
        top = jnp.maximum(top, level)
    total = jnp.zeros((rows, width), jnp.float32)
    share = jnp.zeros((rows, width), jnp.float32)
    for value, level in zip(values, levels):
        factor = jnp.exp(level - top)
        total = total + value * factor
        share = share + factor
    outs[0][...] = (total / share).astype(outs[0].dtype)
    if not final:
        level = top + jnp.log(share)
        if width < 128:
            level = jnp.concatenate([level, level], axis=1)
        write_levels(outs[1], level, heads, head_size)


def merge(parts, rows, head_size, final):
    width = parts[0][0].shape[1]
    operands, in_specs = [], []
    for value, level, block in parts:
        operands += [value, level]
        in_specs += [
            pl.BlockSpec((rows, width), lambda i, block=block: (block, 0)),
            pl.BlockSpec((8, rows), lambda i, block=block: (0, block)),
        ]
    out_shape = [
        jax.ShapeDtypeStruct((rows, width), jnp.bfloat16),
        jax.ShapeDtypeStruct((8, rows), jnp.float32),
    ]
    out_specs = [
        pl.BlockSpec((rows, width), lambda i: (0, 0)),
        pl.BlockSpec((8, rows), lambda i: (0, 0)),
    ]
    keep = 1 if final else 2
    return pl.pallas_call(
        partial(merge_kernel, head_size, len(parts), final),
        grid=(1,),
        out_shape=out_shape[:keep],
        in_specs=in_specs,
        out_specs=out_specs[:keep],
        compiler_params=params(),
        name="merge",
    )(*operands)


def project_kernel(distances, has_total, aged, place_ref, weight_ref, *refs):
    refs = list(refs)
    blocks = [refs.pop(0) for _ in distances]
    total_ref = refs.pop(0) if has_total else None
    if aged:
        aged_ref, out_ref, aged_out, semaphore = refs
        copy = pltpu.make_async_copy(aged_ref, aged_out, semaphore)
        copy.start()
    else:
        (out_ref,) = refs
    place = place_ref[0]
    width = blocks[0].shape[1]
    weights = []
    for distance in distances:
        start = pl.multiple_of((place ^ distance) * width, width)
        weights.append(weight_ref[pl.ds(start, width), :])
    total = jnp.dot(
        jnp.concatenate([block[...] for block in blocks], axis=1),
        jnp.concatenate(weights, axis=0),
        preferred_element_type=jnp.float32,
    )
    if has_total:
        total = total + total_ref[...]
    out_ref[...] = total.astype(out_ref.dtype)
    if aged:
        copy.wait()


def project(place, out_weight, blocks, distances, total=None, aged=None):
    rows, columns = blocks[0].shape[0], out_weight.shape[1]
    operands = [place, out_weight, *blocks]
    in_specs = [pl.BlockSpec(memory_space=SMEM)]
    in_specs += [pl.BlockSpec(memory_space=VMEM)] * (1 + len(blocks))
    dtype = jnp.float32 if total is None else jnp.bfloat16
    out_shape = [jax.ShapeDtypeStruct((rows, columns), dtype)]
    out_specs = [pl.BlockSpec(memory_space=VMEM)]
    scratch = []
    if total is not None:
        operands.append(total)
        in_specs.append(pl.BlockSpec(memory_space=VMEM))
    if aged is not None:
        operands.append(aged)
        in_specs.append(pl.BlockSpec(memory_space=pl.ANY))
        out_shape.append(jax.ShapeDtypeStruct(aged.shape, aged.dtype))
        out_specs.append(pl.BlockSpec(memory_space=pl.ANY))
        scratch.append(pltpu.SemaphoreType.DMA)
    return pl.pallas_call(
        partial(project_kernel, distances, total is not None, aged is not None),
        out_shape=out_shape,
        in_specs=in_specs,
        out_specs=out_specs,
        scratch_shapes=scratch,
        compiler_params=params(),
        cost_estimate=pl.CostEstimate(
            flops=2 * rows * columns * blocks[0].shape[1] * len(blocks),
            bytes_accessed=4 * rows * columns,
            transcendentals=0,
        ),
        name="project",
    )(*operands)


def after(array, *others):
    return lax.optimization_barrier((array, *others))[0]


def local(queries, raw_clip, pool_weight, old_memory, valid_columns, out_weight):
    query_rows, model_width = queries.shape
    head_size = model_width // H
    slots = lax.axis_size("slot")
    spaces = lax.axis_size("space")
    columns = old_memory.shape[3]
    width = model_width // slots
    slot_index = lax.axis_index("slot")
    place = slot_index.astype(jnp.int32).reshape(1)

    own_queries = lax.dynamic_slice_in_dim(queries, slot_index * width, width, axis=1)
    evens = range(2, spaces, 2)
    near = jnp.concatenate([exchange(own_queries, "space", e) for e in evens] + [own_queries], 0)

    resident = old_memory.reshape(-1, old_memory.shape[-1])
    tokens = resident.shape[0]
    half = slots // 2
    pairs = [tuple(range(d, d + 2)) for d in range(0, slots, 2)]
    odd_far = tuple(range(half + 1, slots, 2))
    odd_near = tuple(range(1, half, 2))
    far_out, near_out, *kept = cut(
        place, resident, slots, (odd_far, odd_near) + tuple((d,) for d in range(0, slots, 2))
    )
    far_in = exchange(far_out, "slot", 1)
    near_in = exchange(near_out, "slot", 1)
    sources = [kept[0], near_in[:tokens]]
    distances = [0, 1]
    for d in list(range(half, slots, 2))[::-1] + list(range(2, half, 2)):
        passed, row = (far_in, d - half) if d >= half else (near_in, d)
        row = row // 2 * tokens
        both = jnp.concatenate([kept[d // 2], passed[row : row + tokens]], axis=0)
        sources.append(exchange(both, "slot", d))
        distances += [d, d + 1]

    far = exchange(near, "space", 1)
    behind = from_behind(raw_clip, "space", 1)
    fresh = pool(raw_clip, behind, pool_weight, head_size)
    fresh_rows = fresh.reshape(-1, fresh.shape[-1])
    aged_memory = from_behind(after(old_memory, *sources), "slot", 1)

    call = partial(
        attend,
        place,
        valid_columns,
        sources=[fresh_rows] + sources,
        tokens=tokens,
        distances=(None,) + tuple(distances),
        columns=columns,
        head_size=head_size,
    )
    far_value, far_level = call(queries=far, dtype=jnp.bfloat16)
    core_value = exchange(far_value, "space", 1)
    core_level = exchange(far_level, "space", 1)
    parts = []
    for k, e in enumerate(evens):
        rows = slice(k * query_rows, (k + 1) * query_rows)
        value, level = call(queries=near[rows], dtype=jnp.float32)
        value, level = merge(
            [(value, level, 0), (core_value, core_level, k)], query_rows, head_size, False
        )
        parts.append((exchange(value, "space", e), exchange(level, "space", e), 0))
    value, level = call(queries=own_queries, dtype=jnp.float32)
    value, _ = lax.optimization_barrier((value, aged_memory))
    parts = [(value, level, 0), (core_value, core_level, len(evens))] + parts
    (mixed,) = merge(parts, query_rows, head_size, True)

    blocks = {0: mixed}
    for d in reversed(range(2, slots, 2)):
        blocks[d] = exchange(mixed, "slot", d)
    for d in range(0, slots, 2):
        blocks[d + 1] = exchange(blocks[d], "slot", 1)
    first, second = tuple(range(half)), tuple(range(half, slots))
    (total,) = project(place, out_weight, [blocks[d] for d in first], first)
    attended, aged_memory = project(
        place, out_weight, [blocks[d] for d in second], second, total, aged_memory
    )
    return (attended, fresh, aged_memory)


def solution(mesh):
    return jax.shard_map(
        local,
        mesh=mesh,
        in_specs=(
            P("space", None),
            P(None, "space", None, "slot"),
            P(None, "slot"),
            P("slot", None, "space", None, None),
            P(),
            P(),
        ),
        out_specs=(
            P("space", None),
            P(None, "space", None, "slot"),
            P("slot", None, "space", None, None),
        ),
        check_vma=False,
    )
```

```python
from functools import partial

import jax
import jax.numpy as jnp
from jax import lax
from jax.experimental import pallas as pl
from jax.experimental.pallas import tpu as pltpu
from jax.sharding import PartitionSpec as P

H = 16
MASKED = -1e30
BLOCK = 512
VMEM_LIMIT = 48 * 1024 * 1024
VMEM = pltpu.VMEM
SMEM = pltpu.SMEM


def params(**more):
    return pltpu.CompilerParams(vmem_limit_bytes=VMEM_LIMIT, **more)


def lanes_of(shape):
    return lax.broadcasted_iota(jnp.int32, shape, len(shape) - 1)


def exchange(block, axis, distance):
    size = lax.axis_size(axis)
    return lax.ppermute(block, axis, [(i, i ^ distance) for i in range(size)])


def from_behind(block, axis, distance):
    devices = range(lax.axis_size(axis))
    return lax.ppermute(block, axis, [(i - distance, i) for i in devices if i - distance in devices])


def pool_kernel(head_size, raw_ref, halo_ref, weight_ref, out_ref, rows_ref, slabs):
    frames, rows, columns, channels = raw_ref.shape
    frames_out, columns_out = frames // 2, columns // 2
    pieces, _, _, wide = slabs.shape
    group = lax.broadcasted_iota(jnp.int32, (wide, wide), 0) // head_size
    averaging = jnp.where(
        group == lanes_of((wide, wide)) // head_size, 1.0 / head_size, 0.0
    ).astype(jnp.float32)
    first_row = lax.broadcasted_iota(jnp.int32, (columns_out, wide), 0) == 0
    mean = partial(
        jnp.dot, precision=lax.Precision.HIGHEST, preferred_element_type=jnp.float32
    )
    for piece in range(pieces):
        lanes = slice(piece * wide, (piece + 1) * wide)
        for f in range(frames):
            slabs[piece, 3 * f] = halo_ref[f, 0, :, lanes].astype(jnp.float32)
            slabs[piece, 3 * f + 1] = raw_ref[f, 0, :, lanes].astype(jnp.float32)
            slabs[piece, 3 * f + 2] = raw_ref[f, 1, :, lanes].astype(jnp.float32)
        weight = weight_ref[:, lanes].astype(jnp.float32)
        for f in range(frames_out):
            sums = [jnp.zeros((columns_out, wide), jnp.float32) for _ in range(3)]
            for a in range(3):
                frame = 2 * f + a - 1
                if frame < 0:
                    continue
                for b in range(3):
                    even = slabs[piece, 3 * frame + b, pl.ds(0, columns_out, stride=2), :]
                    odd = slabs[piece, 3 * frame + b, pl.ds(1, columns_out, stride=2), :]
                    for g, tapped in enumerate((odd, even, odd)):
                        tap = 9 * a + 3 * b + g
                        sums[g] = sums[g] + weight[tap : tap + 1] * tapped
            behind = jnp.where(first_row, 0.0, pltpu.roll(sums[0], 1, 0))
            pooled = behind + sums[1] + sums[2]
            centered = pooled - mean(pooled, averaging)
            spread = mean(centered * centered, averaging)
            normed = (centered * lax.rsqrt(spread + 1e-06)).astype(jnp.bfloat16)
            out_ref[f, 0, :, lanes] = normed
            rows_ref[f * columns_out : (f + 1) * columns_out, lanes] = normed


def edge_kernel(raw_ref, out_ref, semaphore):
    rows = raw_ref.shape[1]
    copy = pltpu.make_async_copy(raw_ref.at[:, pl.ds(rows - 1, 1)], out_ref, semaphore)
    copy.start()
    copy.wait()


def edge(raw_clip):
    frames, rows, columns, channels = raw_clip.shape
    return pl.pallas_call(
        edge_kernel,
        out_shape=jax.ShapeDtypeStruct((frames, 1, columns, channels), raw_clip.dtype),
        in_specs=[pl.BlockSpec(memory_space=pl.ANY)],
        out_specs=pl.BlockSpec(memory_space=VMEM),
        scratch_shapes=[pltpu.SemaphoreType.DMA],
        compiler_params=params(),
        name="edge",
    )(raw_clip)


def pool(raw_clip, halo, pool_weight, head_size):
    frames, rows, columns, channels = raw_clip.shape
    return pl.pallas_call(
        partial(pool_kernel, head_size),
        out_shape=[
            jax.ShapeDtypeStruct((frames // 2, 1, columns // 2, channels), jnp.bfloat16),
            jax.ShapeDtypeStruct((frames // 2 * columns // 2, channels), jnp.bfloat16),
        ],
        in_specs=[pl.BlockSpec(memory_space=VMEM)] * 3,
        out_specs=[pl.BlockSpec(memory_space=VMEM)] * 2,
        scratch_shapes=[VMEM((channels // 128, 3 * frames, columns, 128), jnp.float32)],
        compiler_params=params(),
        name="pool",
    )(raw_clip, halo, pool_weight)


def cut_kernel(width, groups, place_ref, memory_ref, *refs):
    out_refs, semaphores = refs[:-1], refs[-1]
    place = place_ref[0]
    tokens = memory_ref.shape[0]
    copies = []
    for group, out_ref in zip(groups, out_refs):
        for k, distance in enumerate(group):
            start = pl.multiple_of((place ^ distance) * width, 128)
            copy = pltpu.make_async_copy(
                memory_ref.at[:, pl.ds(start, width)],
                out_ref.at[pl.ds(k * tokens, tokens)],
                semaphores.at[len(copies)],
            )
            copy.start()
            copies.append(copy)
    for copy in copies:
        copy.wait()


def cut(place, memory, pieces, groups):
    tokens, channels = memory.shape
    width = channels // pieces
    return pl.pallas_call(
        partial(cut_kernel, width, groups),
        out_shape=[jax.ShapeDtypeStruct((len(g) * tokens, width), memory.dtype) for g in groups],
        in_specs=[pl.BlockSpec(memory_space=SMEM), pl.BlockSpec(memory_space=pl.ANY)],
        out_specs=[pl.BlockSpec(memory_space=VMEM)] * len(groups),
        scratch_shapes=[pltpu.SemaphoreType.DMA((pieces,))],
        compiler_params=params(),
        name="cut",
    )(place, memory)


def attend_kernel(
    head_size, columns, tokens, distances, travels, place_ref, valid_ref, query_ref, *refs
):
    outs = 1 if travels else 2
    sources, out_refs = refs[:-outs], refs[-outs:]
    rows, width = query_ref.shape
    heads = width // head_size
    wide = 2 * head_size
    place = place_ref[0]
    biases = []
    column = lanes_of((1, tokens)) % columns
    for distance in distances:
        valid = valid_ref[0] if distance is None else valid_ref[1 + (place ^ distance)]
        biases.append(jnp.where(column < valid, 0.0, MASKED))
    bias = jnp.concatenate(biases, axis=1)
    lane = lanes_of((rows, wide))
    queries = query_ref[...].astype(jnp.float32) * head_size ** (-0.5)
    memory, scores = [], []
    for h in range(heads):
        own = queries if h == 0 else pltpu.roll(queries, width - h * head_size, 1)
        if own.shape[1] < wide:
            own = jnp.concatenate([own, own], axis=1)
        own = jnp.where(lane < head_size, own, 0.0).astype(jnp.bfloat16)
        memory.append(
            jnp.concatenate([source[:, h * wide : (h + 1) * wide] for source in sources], axis=0)
        )
        product = lax.dot_general(
            own, memory[h], (((1,), (1,)), ((), ())), preferred_element_type=jnp.float32
        )
        scores.append(product + bias)
    weights, peaks = [], []
    for h in range(heads):
        peaks.append(jnp.max(scores[h], axis=1, keepdims=True))
        weights.append(jnp.exp(scores[h] - peaks[h]).astype(jnp.bfloat16))
    values, levels = [], []
    memory_lane = lanes_of(memory[0].shape)
    for h in range(heads):
        ones_and_values = jnp.where(memory_lane < head_size, 1.0, memory[h].astype(jnp.float32))
        total = jnp.dot(
            weights[h], ones_and_values.astype(jnp.bfloat16), preferred_element_type=jnp.float32
        )
        turned = pltpu.roll(total, head_size, 1)
        if h % 2:
            values.append(total / turned)
            levels.append(jnp.log(turned) + peaks[h])
        else:
            values.append(turned / total)
            levels.append(jnp.log(total) + peaks[h])
    if heads == 1:
        value, level = values[0][:, :head_size], levels[0]
    else:
        value = jnp.where(lane < head_size, *values)
        level = jnp.where(lane < head_size, *levels)
    if travels:
        pack(out_refs[0], value, level, head_size)
    else:
        out_refs[0][...] = value
        out_refs[1][...] = level[:, :width]


def packed_rows(rows, width, head_size):
    return -(-3 * (width // head_size) * rows // width // 16) * 16


def pack(out_ref, value, level, head_size):
    rows, width = value.shape
    out_ref[:rows] = value.astype(out_ref.dtype)
    turned = level.T
    lines = []
    for h in range(width // head_size):
        rest = turned[h * head_size : h * head_size + 1, :]
        for _ in range(3):
            term = rest.astype(jnp.bfloat16).astype(jnp.float32)
            rest = rest - term
            lines += [term[:, j : j + width] for j in range(0, rows, width)]
    below = packed_rows(rows, width, head_size)
    if len(lines) < below:
        lines.append(jnp.zeros((below - len(lines), width), jnp.float32))
    out_ref[rows:] = jnp.concatenate(lines, axis=0).astype(out_ref.dtype)


def unpack(ref, rows, head_size):
    width = ref.shape[1]
    packed = ref[rows:].astype(jnp.float32)
    count = rows // width
    spread = []
    for h in range(width // head_size):
        first = 3 * h * count
        line = [
            packed[j : j + 1] + packed[j + count : j + count + 1] + packed[j + 2 * count : j + 2 * count + 1]
            for j in range(first, first + count)
        ]
        spread.append(jnp.broadcast_to(jnp.concatenate(line, axis=1), (head_size, rows)))
    return ref[:rows].astype(jnp.float32), jnp.concatenate(spread, axis=0).T


def attend(
    place, valid, queries, sources, tokens, distances, columns, head_size, travels, weight=1
):
    rows, width = queries.shape
    heads = width // head_size
    wide = 2 * head_size
    key_count = sum(source.shape[0] for source in sources)
    block = min(BLOCK, rows)
    if travels:
        held = block + packed_rows(block, width, head_size)
        out_shape = [jax.ShapeDtypeStruct((rows // block * held, width), jnp.bfloat16)]
        out_specs = [pl.BlockSpec((held, width), lambda i: (i, 0))]
    else:
        out_shape = [jax.ShapeDtypeStruct((rows, width), jnp.float32)] * 2
        out_specs = [pl.BlockSpec((block, width), lambda i: (i, 0))] * 2
    return pl.pallas_call(
        partial(attend_kernel, head_size, columns, tokens, distances, travels),
        grid=(rows // block,),
        out_shape=out_shape,
        in_specs=[
            pl.BlockSpec(memory_space=SMEM),
            pl.BlockSpec(memory_space=SMEM),
            pl.BlockSpec((block, width), lambda i: (i, 0)),
        ]
        + [pl.BlockSpec(memory_space=VMEM)] * len(sources),
        out_specs=out_specs,
        compiler_params=params(),
        cost_estimate=pl.CostEstimate(
            flops=weight * 4 * rows * key_count * wide * heads,
            bytes_accessed=4 * key_count * wide * heads + 8 * rows * wide * heads,
            transcendentals=rows * key_count * heads,
        ),
        name="attend",
    )(place, valid, queries, *sources)


def merge_kernel(head_size, travels, value_ref, level_ref, *refs):
    parts, out_ref = refs[:-1], refs[-1]
    rows, width = value_ref.shape
    values, levels = [value_ref[...]], [level_ref[...]]
    for ref in parts:
        value, level = unpack(ref, rows, head_size)
        values.append(value)
        levels.append(level)
    top = levels[0]
    for level in levels[1:]:
        top = jnp.maximum(top, level)
    total = jnp.zeros((rows, width), jnp.float32)
    share = jnp.zeros((rows, width), jnp.float32)
    for value, level in zip(values, levels):
        factor = jnp.exp(level - top)
        total = total + value * factor
        share = share + factor
    mixed = total / share
    if travels:
        level = top + jnp.log(share)
        if width < 128:
            level = jnp.concatenate([level, level], axis=1)
        pack(out_ref, mixed, level, head_size)
    else:
        out_ref[...] = mixed.astype(out_ref.dtype)


def merge(value, level, parts, head_size, travels):
    rows, width = value.shape
    held = rows + packed_rows(rows, width, head_size)
    whole = pl.BlockSpec((rows, width), lambda i: (0, 0))
    part_specs = [pl.BlockSpec((held, width), lambda i, k=k: (k, 0)) for _, k in parts]
    out_rows = held if travels else rows
    return pl.pallas_call(
        partial(merge_kernel, head_size, travels),
        grid=(1,),
        out_shape=jax.ShapeDtypeStruct((out_rows, width), jnp.bfloat16),
        in_specs=[whole, whole] + part_specs,
        out_specs=pl.BlockSpec((out_rows, width), lambda i: (0, 0)),
        compiler_params=params(),
        name="merge",
    )(value, level, *[part for part, _ in parts])


def weight_rows(weight_ref, place, distances, width):
    starts = [pl.multiple_of((place ^ d) * width, width) for d in distances]
    return jnp.concatenate([weight_ref[pl.ds(start, width), :] for start in starts], axis=0)


def project_early_kernel(distances, place_ref, weight_ref, *refs):
    blocks, (aged_ref, out_ref, aged_out, semaphore) = refs[:-4], refs[-4:]
    copy = pltpu.make_async_copy(aged_ref, aged_out, semaphore)
    copy.start()
    out_ref[...] = jnp.dot(
        jnp.concatenate([block[...] for block in blocks], axis=1),
        weight_rows(weight_ref, place_ref[0], distances, blocks[0].shape[1]),
        preferred_element_type=jnp.float32,
    )
    copy.wait()


def project_late_kernel(distances, place_ref, weight_ref, *refs):
    blocks, (total_ref, out_ref, held, semaphores) = refs[:-4], refs[-4:]
    weights = weight_rows(weight_ref, place_ref[0], distances, blocks[0].shape[1])
    rows = total_ref.shape[0]
    step = rows // semaphores.shape[0]
    copies = []
    for k in range(semaphores.shape[0]):
        here = slice(k * step, (k + 1) * step)
        total = total_ref[here] + jnp.dot(
            jnp.concatenate([block[here] for block in blocks], axis=1),
            weights,
            preferred_element_type=jnp.float32,
        )
        held[here] = total.astype(held.dtype)
        copy = pltpu.make_async_copy(
            held.at[pl.ds(k * step, step)], out_ref.at[pl.ds(k * step, step)], semaphores.at[k]
        )
        copy.start()
        copies.append(copy)
    for copy in copies:
        copy.wait()


def project_cost(rows, columns, depth):
    return pl.CostEstimate(
        flops=2 * rows * columns * depth, bytes_accessed=4 * rows * columns, transcendentals=0
    )


def project_early(place, out_weight, blocks, distances, aged):
    rows, columns = blocks[0].shape[0], out_weight.shape[1]
    return pl.pallas_call(
        partial(project_early_kernel, distances),
        out_shape=[
            jax.ShapeDtypeStruct((rows, columns), jnp.float32),
            jax.ShapeDtypeStruct(aged.shape, aged.dtype),
        ],
        in_specs=[pl.BlockSpec(memory_space=SMEM)]
        + [pl.BlockSpec(memory_space=VMEM)] * (1 + len(blocks))
        + [pl.BlockSpec(memory_space=pl.ANY)],
        out_specs=[pl.BlockSpec(memory_space=VMEM), pl.BlockSpec(memory_space=pl.ANY)],
        scratch_shapes=[pltpu.SemaphoreType.DMA],
        compiler_params=params(),
        cost_estimate=project_cost(rows, columns, blocks[0].shape[1] * len(blocks)),
        name="project_early",
    )(place, out_weight, *blocks, aged)


def project_late(place, out_weight, blocks, distances, total):
    rows, columns = total.shape
    return pl.pallas_call(
        partial(project_late_kernel, distances),
        out_shape=jax.ShapeDtypeStruct((rows, columns), jnp.bfloat16),
        in_specs=[pl.BlockSpec(memory_space=SMEM)]
        + [pl.BlockSpec(memory_space=VMEM)] * (2 + len(blocks)),
        out_specs=pl.BlockSpec(memory_space=pl.ANY),
        scratch_shapes=[VMEM((rows, columns), jnp.bfloat16), pltpu.SemaphoreType.DMA((4,))],
        compiler_params=params(),
        cost_estimate=project_cost(rows, columns, blocks[0].shape[1] * len(blocks)),
        name="project_late",
    )(place, out_weight, *blocks, total)


def after(array, *others):
    return lax.optimization_barrier((array, *others))[0]


def gather(mixed, slots, aged):
    half, top = slots // 2, slots - 2
    blocks = {0: mixed, top: exchange(mixed, "slot", top)}
    late = after(mixed, aged)
    blocks[2] = exchange(late, "slot", 2)
    blocks[1] = exchange(late, "slot", 1)
    for d in range(3, half):
        blocks[d] = exchange(blocks[d ^ 1] if d % 2 else late, "slot", 1 if d % 2 else d)
    for d in range(1, half):
        blocks[top ^ d] = exchange(blocks[top], "slot", d)
    return blocks


def local(queries, raw_clip, pool_weight, old_memory, valid_columns, out_weight):
    query_rows, model_width = queries.shape
    head_size = model_width // H
    slots = lax.axis_size("slot")
    spaces = lax.axis_size("space")
    columns = old_memory.shape[3]
    width = model_width // slots
    slot_index = lax.axis_index("slot")
    place = slot_index.astype(jnp.int32).reshape(1)
    half = slots // 2

    own_queries = lax.dynamic_slice_in_dim(queries, slot_index * width, width, axis=1)
    evens = range(2, spaces, 2)
    crossed = {e: exchange(own_queries, "space", e) for e in evens}
    near = jnp.concatenate([crossed[e] for e in evens] + [own_queries], axis=0)

    resident = old_memory.reshape(-1, old_memory.shape[-1])
    tokens = resident.shape[0]
    odd_far = tuple(range(half + 1, slots, 2))
    odd_near = tuple(range(1, half, 2))
    far_out, near_out, *kept = cut(
        place, resident, slots, (odd_far, odd_near) + tuple((d,) for d in range(0, slots, 2))
    )
    far_in = exchange(far_out, "slot", 1)
    near_in = exchange(near_out, "slot", 1)
    sources = {0: kept[0], 1: near_in[:tokens]}
    for d in list(range(half, slots, 2))[::-1]:
        row = (d - half) // 2 * tokens
        both = jnp.concatenate([kept[d // 2], far_in[row : row + tokens]], axis=0)
        both = exchange(both, "slot", d)
        sources[d], sources[d + 1] = both[:tokens], both[tokens:]
    far = exchange(near, "space", 1)
    behind = from_behind(edge(raw_clip), "space", 1)
    fresh, fresh_rows = pool(raw_clip, behind, pool_weight, head_size)
    for d in range(2, half, 2):
        row = d // 2 * tokens
        both = jnp.concatenate([kept[d // 2], near_in[row : row + tokens]], axis=0)
        both = exchange(after(both, fresh_rows), "slot", d)
        sources[d], sources[d + 1] = both[:tokens], both[tokens:]
    call = partial(
        attend,
        place,
        valid_columns,
        sources=[fresh_rows] + [sources[d] for d in range(slots)],
        tokens=tokens,
        distances=(None,) + tuple(range(slots)),
        columns=columns,
        head_size=head_size,
    )
    aged_memory = from_behind(after(old_memory, *sources.values()), "slot", 1)
    parts = []
    for k, e in enumerate(evens):
        rows = slice(k * query_rows, (k + 1) * query_rows)
        (part,) = call(queries=far[rows], travels=True)
        core_part = exchange(part, "space", 1)
        value, level = call(queries=near[rows], travels=False)
        part = merge(value, level, [(core_part, 0)], head_size, True)
        parts.append((exchange(part, "space", e), 0))
        sent_part = part
    (part,) = call(queries=after(far[len(evens) * query_rows :], sent_part), travels=True)
    parts.append((exchange(part, "space", 1), 0))
    value, level = call(queries=own_queries, travels=False, weight=4)
    mixed = merge(value, level, parts, head_size, False)

    blocks = gather(mixed, slots, aged_memory)
    first, second = tuple(range(half)), tuple(range(half, slots))
    total, aged_memory = project_early(
        place, out_weight, [blocks[d] for d in first], first, aged_memory
    )
    attended = project_late(place, out_weight, [blocks[d] for d in second], second, total)
    return (attended, fresh, aged_memory)


def solution(mesh):
    return jax.shard_map(
        local,
        mesh=mesh,
        in_specs=(
            P("space", None),
            P(None, "space", None, "slot"),
            P(None, "slot"),
            P("slot", None, "space", None, None),
            P(),
            P(),
        ),
        out_specs=(
            P("space", None),
            P(None, "space", None, "slot"),
            P("slot", None, "space", None, None),
        ),
        check_vma=False,
    )
```

```python
from functools import partial

import jax
import jax.numpy as jnp
from jax import lax
from jax.experimental import pallas as pl
from jax.experimental.pallas import tpu as pltpu
from jax.sharding import PartitionSpec as P

H = 16
MASKED = -1e30
BLOCK = 512
VMEM_LIMIT = 48 * 1024 * 1024
VMEM = pltpu.VMEM
SMEM = pltpu.SMEM


def params(**more):
    return pltpu.CompilerParams(vmem_limit_bytes=VMEM_LIMIT, **more)


def lanes_of(shape):
    return lax.broadcasted_iota(jnp.int32, shape, len(shape) - 1)


def exchange(block, axis, distance):
    size = lax.axis_size(axis)
    return lax.ppermute(block, axis, [(i, i ^ distance) for i in range(size)])


def from_behind(block, axis, distance):
    devices = range(lax.axis_size(axis))
    return lax.ppermute(block, axis, [(i - distance, i) for i in devices if i - distance in devices])


def pool_kernel(head_size, raw_ref, halo_ref, weight_ref, out_ref, rows_ref, slabs):
    frames, rows, columns, channels = raw_ref.shape
    frames_out, columns_out = frames // 2, columns // 2
    pieces, _, _, wide = slabs.shape
    group = lax.broadcasted_iota(jnp.int32, (wide, wide), 0) // head_size
    averaging = jnp.where(
        group == lanes_of((wide, wide)) // head_size, 1.0 / head_size, 0.0
    ).astype(jnp.float32)
    first_row = lax.broadcasted_iota(jnp.int32, (columns_out, wide), 0) == 0
    mean = partial(
        jnp.dot, precision=lax.Precision.HIGHEST, preferred_element_type=jnp.float32
    )
    for piece in range(pieces):
        lanes = slice(piece * wide, (piece + 1) * wide)
        for f in range(frames):
            slabs[piece, 3 * f] = halo_ref[f, 0, :, lanes].astype(jnp.float32)
            slabs[piece, 3 * f + 1] = raw_ref[f, 0, :, lanes].astype(jnp.float32)
            slabs[piece, 3 * f + 2] = raw_ref[f, 1, :, lanes].astype(jnp.float32)
        weight = weight_ref[:, lanes].astype(jnp.float32)
        for f in range(frames_out):
            sums = [jnp.zeros((columns_out, wide), jnp.float32) for _ in range(3)]
            for a in range(3):
                frame = 2 * f + a - 1
                if frame < 0:
                    continue
                for b in range(3):
                    even = slabs[piece, 3 * frame + b, pl.ds(0, columns_out, stride=2), :]
                    odd = slabs[piece, 3 * frame + b, pl.ds(1, columns_out, stride=2), :]
                    for g, tapped in enumerate((odd, even, odd)):
                        tap = 9 * a + 3 * b + g
                        sums[g] = sums[g] + weight[tap : tap + 1] * tapped
            behind = jnp.where(first_row, 0.0, pltpu.roll(sums[0], 1, 0))
            pooled = behind + sums[1] + sums[2]
            centered = pooled - mean(pooled, averaging)
            spread = mean(centered * centered, averaging)
            normed = (centered * lax.rsqrt(spread + 1e-06)).astype(jnp.bfloat16)
            out_ref[f, 0, :, lanes] = normed
            rows_ref[f * columns_out : (f + 1) * columns_out, lanes] = normed


def edge_kernel(raw_ref, out_ref, semaphore):
    rows = raw_ref.shape[1]
    copy = pltpu.make_async_copy(raw_ref.at[:, pl.ds(rows - 1, 1)], out_ref, semaphore)
    copy.start()
    copy.wait()


def edge(raw_clip):
    frames, rows, columns, channels = raw_clip.shape
    return pl.pallas_call(
        edge_kernel,
        out_shape=jax.ShapeDtypeStruct((frames, 1, columns, channels), raw_clip.dtype),
        in_specs=[pl.BlockSpec(memory_space=pl.ANY)],
        out_specs=pl.BlockSpec(memory_space=VMEM),
        scratch_shapes=[pltpu.SemaphoreType.DMA],
        compiler_params=params(),
        name="edge",
    )(raw_clip)


def pool(raw_clip, halo, pool_weight, head_size):
    frames, rows, columns, channels = raw_clip.shape
    return pl.pallas_call(
        partial(pool_kernel, head_size),
        out_shape=[
            jax.ShapeDtypeStruct((frames // 2, 1, columns // 2, channels), jnp.bfloat16),
            jax.ShapeDtypeStruct((frames // 2 * columns // 2, channels), jnp.bfloat16),
        ],
        in_specs=[pl.BlockSpec(memory_space=VMEM)] * 3,
        out_specs=[pl.BlockSpec(memory_space=VMEM)] * 2,
        scratch_shapes=[VMEM((channels // 128, 3 * frames, columns, 128), jnp.float32)],
        compiler_params=params(),
        name="pool",
    )(raw_clip, halo, pool_weight)


def cut_kernel(width, groups, place_ref, memory_ref, *refs):
    out_refs, semaphores = refs[:-1], refs[-1]
    place = place_ref[0]
    tokens = memory_ref.shape[0]
    copies = []
    for group, out_ref in zip(groups, out_refs):
        for k, distance in enumerate(group):
            start = pl.multiple_of((place ^ distance) * width, 128)
            copy = pltpu.make_async_copy(
                memory_ref.at[:, pl.ds(start, width)],
                out_ref.at[pl.ds(k * tokens, tokens)],
                semaphores.at[len(copies)],
            )
            copy.start()
            copies.append(copy)
    for copy in copies:
        copy.wait()


def cut(place, memory, pieces, groups):
    tokens, channels = memory.shape
    width = channels // pieces
    return pl.pallas_call(
        partial(cut_kernel, width, groups),
        out_shape=[jax.ShapeDtypeStruct((len(g) * tokens, width), memory.dtype) for g in groups],
        in_specs=[pl.BlockSpec(memory_space=SMEM), pl.BlockSpec(memory_space=pl.ANY)],
        out_specs=[pl.BlockSpec(memory_space=VMEM)] * len(groups),
        scratch_shapes=[pltpu.SemaphoreType.DMA((pieces,))],
        compiler_params=params(),
        name="cut",
    )(place, memory)


def mask_kernel(columns, tokens, distances, place_ref, valid_ref, out_ref):
    place = place_ref[0]
    column = lanes_of((out_ref.shape[0], tokens)) % columns
    for k, distance in enumerate(distances):
        valid = valid_ref[0] if distance is None else valid_ref[1 + (place ^ distance)]
        bias = jnp.where(column < valid, 0.0, MASKED)
        out_ref[:, k * tokens : (k + 1) * tokens] = bias


def mask(place, valid, columns, tokens, distances):
    return pl.pallas_call(
        partial(mask_kernel, columns, tokens, distances),
        out_shape=jax.ShapeDtypeStruct((8, tokens * len(distances)), jnp.float32),
        in_specs=[pl.BlockSpec(memory_space=SMEM)] * 2,
        out_specs=pl.BlockSpec(memory_space=VMEM),
        compiler_params=params(),
        name="mask",
    )(place, valid)


def attend_kernel(
    head_size, travels, bias_ref, query_ref, *refs
):
    outs = 1 if travels else 2
    sources, out_refs = refs[:-outs], refs[-outs:]
    rows, width = query_ref.shape
    heads = width // head_size
    wide = 2 * head_size
    lane = lanes_of((rows, wide))
    queries = query_ref[...].astype(jnp.float32) * head_size ** (-0.5)
    memory, scores = [], []
    for h in range(heads):
        own = queries if h == 0 else pltpu.roll(queries, width - h * head_size, 1)
        if own.shape[1] < wide:
            own = jnp.concatenate([own, own], axis=1)
        own = jnp.where(lane < head_size, own, 0.0).astype(jnp.bfloat16)
        memory.append(
            jnp.concatenate([source[:, h * wide : (h + 1) * wide] for source in sources], axis=0)
        )
        product = lax.dot_general(
            own, memory[h], (((1,), (1,)), ((), ())), preferred_element_type=jnp.float32
        )
        scores.append(product + bias_ref[:1])
    weights, peaks = [], []
    for h in range(heads):
        peaks.append(jnp.max(scores[h], axis=1, keepdims=True))
        weights.append(jnp.exp(scores[h] - peaks[h]).astype(jnp.bfloat16))
    totals = []
    memory_lane = lanes_of(memory[0].shape)
    for h in range(heads):
        ones_and_values = jnp.where(memory_lane < head_size, 1.0, memory[h].astype(jnp.float32))
        total = jnp.dot(
            weights[h], ones_and_values.astype(jnp.bfloat16), preferred_element_type=jnp.float32
        )
        totals.append(total)
    if heads == 1:
        turned = pltpu.roll(totals[0], head_size, 1)
        value = (turned / totals[0])[:, :head_size]
        level = jnp.log(totals[0]) + peaks[0]
    else:
        first = lane < head_size
        sums = jnp.where(first, totals[0], pltpu.roll(totals[1], head_size, 1))
        value = jnp.where(first, pltpu.roll(totals[0], head_size, 1), totals[1]) / sums
        level = jnp.log(sums) + jnp.where(first, peaks[0], peaks[1])
    if travels:
        pack(out_refs[0], value, level, head_size)
    else:
        out_refs[0][...] = value
        out_refs[1][...] = level[:, :width]


def packed_rows(rows, width, head_size):
    return -(-3 * (width // head_size) * rows // width // 16) * 16


def pack(out_ref, value, level, head_size):
    rows, width = value.shape
    out_ref[:rows] = value.astype(out_ref.dtype)
    turned = level.T
    lines = []
    for h in range(width // head_size):
        rest = turned[h * head_size : h * head_size + 1, :]
        for _ in range(3):
            term = rest.astype(jnp.bfloat16).astype(jnp.float32)
            rest = rest - term
            lines += [term[:, j : j + width] for j in range(0, rows, width)]
    below = packed_rows(rows, width, head_size)
    if len(lines) < below:
        lines.append(jnp.zeros((below - len(lines), width), jnp.float32))
    out_ref[rows:] = jnp.concatenate(lines, axis=0).astype(out_ref.dtype)


def unpack(ref, rows, head_size):
    width = ref.shape[1]
    packed = ref[rows:].astype(jnp.float32)
    count = rows // width
    spread = []
    for h in range(width // head_size):
        first = 3 * h * count
        line = [
            packed[j : j + 1] + packed[j + count : j + count + 1] + packed[j + 2 * count : j + 2 * count + 1]
            for j in range(first, first + count)
        ]
        spread.append(jnp.broadcast_to(jnp.concatenate(line, axis=1), (head_size, rows)))
    return ref[:rows].astype(jnp.float32), jnp.concatenate(spread, axis=0).T


def attend(
    bias, queries, sources, head_size, travels, weight=1
):
    rows, width = queries.shape
    heads = width // head_size
    wide = 2 * head_size
    key_count = sum(source.shape[0] for source in sources)
    block = min(BLOCK, rows)
    if travels:
        held = block + packed_rows(block, width, head_size)
        out_shape = [jax.ShapeDtypeStruct((rows // block * held, width), jnp.bfloat16)]
        out_specs = [pl.BlockSpec((held, width), lambda i: (i, 0))]
    else:
        out_shape = [jax.ShapeDtypeStruct((rows, width), jnp.float32)] * 2
        out_specs = [pl.BlockSpec((block, width), lambda i: (i, 0))] * 2
    return pl.pallas_call(
        partial(attend_kernel, head_size, travels),
        grid=(rows // block,),
        out_shape=out_shape,
        in_specs=[
            pl.BlockSpec(memory_space=VMEM),
            pl.BlockSpec((block, width), lambda i: (i, 0)),
        ]
        + [pl.BlockSpec(memory_space=VMEM)] * len(sources),
        out_specs=out_specs,
        compiler_params=params(),
        cost_estimate=pl.CostEstimate(
            flops=weight * 4 * rows * key_count * wide * heads,
            bytes_accessed=4 * key_count * wide * heads + 8 * rows * wide * heads,
            transcendentals=rows * key_count * heads,
        ),
        name="attend",
    )(bias, queries, *sources)


def merge_kernel(head_size, travels, value_ref, level_ref, *refs):
    parts, out_ref = refs[:-1], refs[-1]
    rows, width = value_ref.shape
    values, levels = [value_ref[...]], [level_ref[...]]
    for ref in parts:
        value, level = unpack(ref, rows, head_size)
        values.append(value)
        levels.append(level)
    top = levels[0]
    for level in levels[1:]:
        top = jnp.maximum(top, level)
    total = jnp.zeros((rows, width), jnp.float32)
    share = jnp.zeros((rows, width), jnp.float32)
    for value, level in zip(values, levels):
        factor = jnp.exp(level - top)
        total = total + value * factor
        share = share + factor
    mixed = total / share
    if travels:
        level = top + jnp.log(share)
        if width < 128:
            level = jnp.concatenate([level, level], axis=1)
        pack(out_ref, mixed, level, head_size)
    else:
        out_ref[...] = mixed.astype(out_ref.dtype)


def merge(value, level, parts, head_size, travels):
    rows, width = value.shape
    held = rows + packed_rows(rows, width, head_size)
    whole = pl.BlockSpec((rows, width), lambda i: (0, 0))
    part_specs = [pl.BlockSpec((held, width), lambda i, k=k: (k, 0)) for _, k in parts]
    out_rows = held if travels else rows
    return pl.pallas_call(
        partial(merge_kernel, head_size, travels),
        grid=(1,),
        out_shape=jax.ShapeDtypeStruct((out_rows, width), jnp.bfloat16),
        in_specs=[whole, whole] + part_specs,
        out_specs=pl.BlockSpec((out_rows, width), lambda i: (0, 0)),
        compiler_params=params(),
        name="merge",
    )(value, level, *[part for part, _ in parts])


def arrange_kernel(place_ref, weight_ref, early_ref, late_ref, semaphores):
    place = place_ref[0]
    count = semaphores.shape[0]
    width = weight_ref.shape[0] // count
    half = count // 2
    copies = []
    for distance in range(count):
        start = pl.multiple_of((place ^ distance) * width, width)
        out_ref = early_ref if distance < half else late_ref
        copy = pltpu.make_async_copy(
            weight_ref.at[pl.ds(start, width)],
            out_ref.at[pl.ds(distance % half * width, width)],
            semaphores.at[distance],
        )
        copy.start()
        copies.append(copy)
    for copy in copies:
        copy.wait()


def arrange(place, out_weight, count):
    depth, columns = out_weight.shape
    return pl.pallas_call(
        arrange_kernel,
        out_shape=[jax.ShapeDtypeStruct((depth // 2, columns), out_weight.dtype)] * 2,
        in_specs=[pl.BlockSpec(memory_space=SMEM), pl.BlockSpec(memory_space=pl.ANY)],
        out_specs=[pl.BlockSpec(memory_space=VMEM)] * 2,
        scratch_shapes=[pltpu.SemaphoreType.DMA((count,))],
        compiler_params=params(),
        name="arrange",
    )(place, out_weight)


def project_early_kernel(weight_ref, *refs):
    blocks, (aged_ref, out_ref, aged_out, semaphore) = refs[:-4], refs[-4:]
    copy = pltpu.make_async_copy(aged_ref, aged_out, semaphore)
    copy.start()
    out_ref[...] = jnp.dot(
        jnp.concatenate([block[...] for block in blocks], axis=1),
        weight_ref[...],
        preferred_element_type=jnp.float32,
    )
    copy.wait()


def project_late_kernel(weight_ref, *refs):
    blocks, (total_ref, out_ref, held, semaphores) = refs[:-4], refs[-4:]
    rows = total_ref.shape[0]
    step = rows // semaphores.shape[0]
    copies = []
    for k in range(semaphores.shape[0]):
        here = slice(k * step, (k + 1) * step)
        total = total_ref[here] + jnp.dot(
            jnp.concatenate([block[here] for block in blocks], axis=1),
            weight_ref[...],
            preferred_element_type=jnp.float32,
        )
        held[here] = total.astype(held.dtype)
        copy = pltpu.make_async_copy(
            held.at[pl.ds(k * step, step)], out_ref.at[pl.ds(k * step, step)], semaphores.at[k]
        )
        copy.start()
        copies.append(copy)
    for copy in copies:
        copy.wait()


def project_cost(rows, columns, depth):
    return pl.CostEstimate(
        flops=2 * rows * columns * depth, bytes_accessed=4 * rows * columns, transcendentals=0
    )


def project_early(out_weight, blocks, aged):
    rows, columns = blocks[0].shape[0], out_weight.shape[1]
    return pl.pallas_call(
        project_early_kernel,
        out_shape=[
            jax.ShapeDtypeStruct((rows, columns), jnp.float32),
            jax.ShapeDtypeStruct(aged.shape, aged.dtype),
        ],
        in_specs=[pl.BlockSpec(memory_space=VMEM)] * (1 + len(blocks))
        + [pl.BlockSpec(memory_space=pl.ANY)],
        out_specs=[pl.BlockSpec(memory_space=VMEM), pl.BlockSpec(memory_space=pl.ANY)],
        scratch_shapes=[pltpu.SemaphoreType.DMA],
        compiler_params=params(),
        cost_estimate=project_cost(rows, columns, blocks[0].shape[1] * len(blocks)),
        name="project_early",
    )(out_weight, *blocks, aged)


def project_late(out_weight, blocks, total):
    rows, columns = total.shape
    return pl.pallas_call(
        project_late_kernel,
        out_shape=jax.ShapeDtypeStruct((rows, columns), jnp.bfloat16),
        in_specs=[pl.BlockSpec(memory_space=VMEM)] * (2 + len(blocks)),
        out_specs=pl.BlockSpec(memory_space=pl.ANY),
        scratch_shapes=[VMEM((rows, columns), jnp.bfloat16), pltpu.SemaphoreType.DMA((4,))],
        compiler_params=params(),
        cost_estimate=project_cost(rows, columns, blocks[0].shape[1] * len(blocks)),
        name="project_late",
    )(out_weight, *blocks, total)


def after(array, *others):
    return lax.optimization_barrier((array, *others))[0]


def gather(mixed, slots, aged):
    half, top = slots // 2, slots - 2
    blocks = {0: mixed, top: exchange(mixed, "slot", top)}
    late = after(mixed, aged)
    blocks[2] = exchange(late, "slot", 2)
    blocks[1] = exchange(late, "slot", 1)
    for d in range(3, half):
        blocks[d] = exchange(late, "slot", d)
    for d in range(1, half):
        blocks[top ^ d] = exchange(blocks[top], "slot", d)
    return blocks


def local(queries, raw_clip, pool_weight, old_memory, valid_columns, out_weight):
    query_rows, model_width = queries.shape
    head_size = model_width // H
    slots = lax.axis_size("slot")
    spaces = lax.axis_size("space")
    columns = old_memory.shape[3]
    width = model_width // slots
    slot_index = lax.axis_index("slot")
    place = slot_index.astype(jnp.int32).reshape(1)
    half = slots // 2

    own_queries = lax.dynamic_slice_in_dim(queries, slot_index * width, width, axis=1)
    evens = range(2, spaces, 2)
    crossed = {e: exchange(own_queries, "space", e) for e in evens}
    near = jnp.concatenate([crossed[e] for e in evens] + [own_queries], axis=0)

    resident = old_memory.reshape(-1, old_memory.shape[-1])
    tokens = resident.shape[0]
    odd_far = tuple(range(half + 1, slots, 2))
    odd_near = tuple(range(1, half, 2))
    far_out, near_out, *kept = cut(
        place, resident, slots, (odd_far, odd_near) + tuple((d,) for d in range(0, slots, 2))
    )
    far_in = exchange(far_out, "slot", 1)
    near_in = exchange(after(near_out, far_in), "slot", 1)
    sources = {0: kept[0], 1: near_in[:tokens]}
    for d in list(range(half, slots, 2))[::-1]:
        row = (d - half) // 2 * tokens
        both = jnp.concatenate([kept[d // 2], far_in[row : row + tokens]], axis=0)
        both = exchange(both, "slot", d)
        sources[d], sources[d + 1] = both[:tokens], both[tokens:]
    behind = from_behind(edge(after(raw_clip, near_in)), "space", 1)
    fresh, fresh_rows = pool(raw_clip, behind, pool_weight, head_size)
    for d in range(2, half, 2):
        row = d // 2 * tokens
        both = jnp.concatenate([kept[d // 2], near_in[row : row + tokens]], axis=0)
        both = exchange(both, "slot", d)
        sources[d], sources[d + 1] = both[:tokens], both[tokens:]
    order = (None,) + tuple(range(slots))
    bias = mask(place, after(valid_columns, fresh_rows), columns, tokens, order)
    far = exchange(after(near, bias), "space", 1)
    aged_memory = from_behind(after(old_memory, *sources.values(), bias), "slot", 1)
    call = partial(
        attend,
        bias,
        sources=[fresh_rows] + [sources[d] for d in range(slots)],
        head_size=head_size,
    )
    parts = []
    for k, e in enumerate(evens):
        rows = slice(k * query_rows, (k + 1) * query_rows)
        (part,) = call(queries=far[rows], travels=True)
        core_part = exchange(part, "space", 1)
        value, level = call(queries=near[rows], travels=False)
        part = merge(value, level, [(core_part, 0)], head_size, True)
        parts.append((exchange(part, "space", e), 0))
        sent_part = part
    (part,) = call(queries=after(far[len(evens) * query_rows :], sent_part), travels=True)
    parts.append((exchange(part, "space", 1), 0))
    value, level = call(queries=own_queries, travels=False, weight=4)
    mixed = merge(value, level, parts, head_size, False)

    blocks = gather(mixed, slots, aged_memory)
    early_weight, late_weight = arrange(place, out_weight, slots)
    total, aged_memory = project_early(early_weight, [blocks[d] for d in range(half)], aged_memory)
    attended = project_late(late_weight, [blocks[d] for d in range(half, slots)], total)
    return (attended, fresh, aged_memory)


def solution(mesh):
    return jax.shard_map(
        local,
        mesh=mesh,
        in_specs=(
            P("space", None),
            P(None, "space", None, "slot"),
            P(None, "slot"),
            P("slot", None, "space", None, None),
            P(),
            P(),
        ),
        out_specs=(
            P("space", None),
            P(None, "space", None, "slot"),
            P("slot", None, "space", None, None),
        ),
        check_vma=False,
    )
```

```python
from functools import partial

import jax
import jax.numpy as jnp
from jax import lax
from jax.experimental import pallas as pl
from jax.experimental.pallas import tpu as pltpu
from jax.sharding import PartitionSpec as P

H = 16
MASKED = -1e30
BLOCK = 512
VMEM_LIMIT = 48 * 1024 * 1024
VMEM = pltpu.VMEM
SMEM = pltpu.SMEM


def params(**more):
    return pltpu.CompilerParams(vmem_limit_bytes=VMEM_LIMIT, **more)


def lanes_of(shape):
    return lax.broadcasted_iota(jnp.int32, shape, len(shape) - 1)


def exchange(block, axis, distance):
    size = lax.axis_size(axis)
    return lax.ppermute(block, axis, [(i, i ^ distance) for i in range(size)])


def from_behind(block, axis, distance):
    devices = range(lax.axis_size(axis))
    return lax.ppermute(block, axis, [(i - distance, i) for i in devices if i - distance in devices])


def pool_kernel(head_size, raw_ref, halo_ref, weight_ref, out_ref, rows_ref, slabs):
    frames, rows, columns, channels = raw_ref.shape
    frames_out, columns_out = frames // 2, columns // 2
    pieces, _, _, wide = slabs.shape
    group = lax.broadcasted_iota(jnp.int32, (wide, wide), 0) // head_size
    averaging = jnp.where(
        group == lanes_of((wide, wide)) // head_size, 1.0 / head_size, 0.0
    ).astype(jnp.float32)
    first_row = lax.broadcasted_iota(jnp.int32, (columns_out, wide), 0) == 0
    mean = partial(
        jnp.dot, precision=lax.Precision.HIGHEST, preferred_element_type=jnp.float32
    )
    for piece in range(pieces):
        lanes = slice(piece * wide, (piece + 1) * wide)
        for f in range(frames):
            slabs[piece, 3 * f] = halo_ref[f, 0, :, lanes].astype(jnp.float32)
            slabs[piece, 3 * f + 1] = raw_ref[f, 0, :, lanes].astype(jnp.float32)
            slabs[piece, 3 * f + 2] = raw_ref[f, 1, :, lanes].astype(jnp.float32)
        weight = weight_ref[:, lanes].astype(jnp.float32)
        for f in range(frames_out):
            sums = [jnp.zeros((columns_out, wide), jnp.float32) for _ in range(3)]
            for a in range(3):
                frame = 2 * f + a - 1
                if frame < 0:
                    continue
                for b in range(3):
                    even = slabs[piece, 3 * frame + b, pl.ds(0, columns_out, stride=2), :]
                    odd = slabs[piece, 3 * frame + b, pl.ds(1, columns_out, stride=2), :]
                    for g, tapped in enumerate((odd, even, odd)):
                        tap = 9 * a + 3 * b + g
                        sums[g] = sums[g] + weight[tap : tap + 1] * tapped
            behind = jnp.where(first_row, 0.0, pltpu.roll(sums[0], 1, 0))
            pooled = behind + sums[1] + sums[2]
            centered = pooled - mean(pooled, averaging)
            spread = mean(centered * centered, averaging)
            normed = (centered * lax.rsqrt(spread + 1e-06)).astype(jnp.bfloat16)
            out_ref[f, 0, :, lanes] = normed
            rows_ref[f * columns_out : (f + 1) * columns_out, lanes] = normed


def edge_kernel(raw_ref, out_ref, semaphore):
    rows = raw_ref.shape[1]
    copy = pltpu.make_async_copy(raw_ref.at[:, pl.ds(rows - 1, 1)], out_ref, semaphore)
    copy.start()
    copy.wait()


def edge(raw_clip):
    frames, rows, columns, channels = raw_clip.shape
    return pl.pallas_call(
        edge_kernel,
        out_shape=jax.ShapeDtypeStruct((frames, 1, columns, channels), raw_clip.dtype),
        in_specs=[pl.BlockSpec(memory_space=pl.ANY)],
        out_specs=pl.BlockSpec(memory_space=VMEM),
        scratch_shapes=[pltpu.SemaphoreType.DMA],
        compiler_params=params(),
        name="edge",
    )(raw_clip)


def pool(raw_clip, halo, pool_weight, head_size):
    frames, rows, columns, channels = raw_clip.shape
    return pl.pallas_call(
        partial(pool_kernel, head_size),
        out_shape=[
            jax.ShapeDtypeStruct((frames // 2, 1, columns // 2, channels), jnp.bfloat16),
            jax.ShapeDtypeStruct((frames // 2 * columns // 2, channels), jnp.bfloat16),
        ],
        in_specs=[pl.BlockSpec(memory_space=VMEM)] * 3,
        out_specs=[pl.BlockSpec(memory_space=VMEM)] * 2,
        scratch_shapes=[VMEM((channels // 128, 3 * frames, columns, 128), jnp.float32)],
        compiler_params=params(),
        name="pool",
    )(raw_clip, halo, pool_weight)


def cut_kernel(width, groups, place_ref, memory_ref, *refs):
    out_refs, semaphores = refs[:-1], refs[-1]
    place = place_ref[0]
    tokens = memory_ref.shape[0]
    copies = []
    for group, out_ref in zip(groups, out_refs):
        for k, distance in enumerate(group):
            start = pl.multiple_of((place ^ distance) * width, 128)
            copy = pltpu.make_async_copy(
                memory_ref.at[:, pl.ds(start, width)],
                out_ref.at[pl.ds(k * tokens, tokens)],
                semaphores.at[len(copies)],
            )
            copy.start()
            copies.append(copy)
    for copy in copies:
        copy.wait()


def cut(place, memory, pieces, groups):
    tokens, channels = memory.shape
    width = channels // pieces
    return pl.pallas_call(
        partial(cut_kernel, width, groups),
        out_shape=[jax.ShapeDtypeStruct((len(g) * tokens, width), memory.dtype) for g in groups],
        in_specs=[pl.BlockSpec(memory_space=SMEM), pl.BlockSpec(memory_space=pl.ANY)],
        out_specs=[pl.BlockSpec(memory_space=VMEM)] * len(groups),
        scratch_shapes=[pltpu.SemaphoreType.DMA((pieces,))],
        compiler_params=params(),
        name="cut",
    )(place, memory)


def mask_kernel(columns, tokens, distances, place_ref, valid_ref, out_ref):
    place = place_ref[0]
    column = lanes_of((out_ref.shape[0], tokens)) % columns
    for k, distance in enumerate(distances):
        valid = valid_ref[0] if distance is None else valid_ref[1 + (place ^ distance)]
        bias = jnp.where(column < valid, 0.0, MASKED)
        out_ref[:, k * tokens : (k + 1) * tokens] = bias


def mask(place, valid, columns, tokens, distances):
    return pl.pallas_call(
        partial(mask_kernel, columns, tokens, distances),
        out_shape=jax.ShapeDtypeStruct((8, tokens * len(distances)), jnp.float32),
        in_specs=[pl.BlockSpec(memory_space=SMEM)] * 2,
        out_specs=pl.BlockSpec(memory_space=VMEM),
        compiler_params=params(),
        name="mask",
    )(place, valid)


def attend_kernel(
    head_size, travels, bias_ref, query_ref, *refs
):
    outs = 1 if travels else 2
    sources, out_refs = refs[:-outs], refs[-outs:]
    rows, width = query_ref.shape
    heads = width // head_size
    wide = 2 * head_size
    lane = lanes_of((rows, wide))
    queries = query_ref[...].astype(jnp.float32) * head_size ** (-0.5)
    groups = [sources[: len(sources) // 2 + 1], sources[len(sources) // 2 + 1 :]]
    memory, scores = [], []
    for h in range(heads):
        own = queries if h == 0 else pltpu.roll(queries, width - h * head_size, 1)
        if own.shape[1] < wide:
            own = jnp.concatenate([own, own], axis=1)
        own = jnp.where(lane < head_size, own, 0.0).astype(jnp.bfloat16)
        memory.append([])
        scores.append([])
        at = 0
        for group in groups:
            held = [source[:, h * wide : (h + 1) * wide] for source in group]
            memory[h].append(jnp.concatenate(held, axis=0))
            product = lax.dot_general(
                own, memory[h][-1], (((1,), (1,)), ((), ())), preferred_element_type=jnp.float32
            )
            count = product.shape[1]
            scores[h].append(product + bias_ref[:1, at : at + count])
            at += count
    weights, peaks = [], []
    for h in range(heads):
        peak = jnp.max(scores[h][0], axis=1, keepdims=True)
        for part in scores[h][1:]:
            peak = jnp.maximum(peak, jnp.max(part, axis=1, keepdims=True))
        peaks.append(peak)
        weights.append([jnp.exp(part - peak).astype(jnp.bfloat16) for part in scores[h]])
    totals = []
    for h in range(heads):
        total = None
        for held, weight in zip(memory[h], weights[h]):
            ones_and_values = jnp.where(lanes_of(held.shape) < head_size, 1.0, held.astype(jnp.float32))
            term = jnp.dot(
                weight, ones_and_values.astype(jnp.bfloat16), preferred_element_type=jnp.float32
            )
            total = term if total is None else total + term
        totals.append(total)
    if heads == 1:
        turned = pltpu.roll(totals[0], head_size, 1)
        value = (turned / totals[0])[:, :head_size]
        level = jnp.log(totals[0]) + peaks[0]
    else:
        first = lane < head_size
        sums = jnp.where(first, totals[0], pltpu.roll(totals[1], head_size, 1))
        value = jnp.where(first, pltpu.roll(totals[0], head_size, 1), totals[1]) / sums
        level = jnp.log(sums) + jnp.where(first, peaks[0], peaks[1])
    if travels:
        pack(out_refs[0], value, level, head_size)
    else:
        out_refs[0][...] = value
        out_refs[1][...] = level[:, :width]


def packed_rows(rows, width, head_size):
    return -(-3 * (width // head_size) * rows // width // 16) * 16


def pack(out_ref, value, level, head_size):
    rows, width = value.shape
    out_ref[:rows] = value.astype(out_ref.dtype)
    turned = level.T
    lines = []
    for h in range(width // head_size):
        rest = turned[h * head_size : h * head_size + 1, :]
        for _ in range(3):
            term = rest.astype(jnp.bfloat16).astype(jnp.float32)
            rest = rest - term
            lines += [term[:, j : j + width] for j in range(0, rows, width)]
    below = packed_rows(rows, width, head_size)
    if len(lines) < below:
        lines.append(jnp.zeros((below - len(lines), width), jnp.float32))
    out_ref[rows:] = jnp.concatenate(lines, axis=0).astype(out_ref.dtype)


def unpack(ref, rows, head_size):
    width = ref.shape[1]
    packed = ref[rows:].astype(jnp.float32)
    count = rows // width
    spread = []
    for h in range(width // head_size):
        first = 3 * h * count
        line = [
            packed[j : j + 1] + packed[j + count : j + count + 1] + packed[j + 2 * count : j + 2 * count + 1]
            for j in range(first, first + count)
        ]
        spread.append(jnp.broadcast_to(jnp.concatenate(line, axis=1), (head_size, rows)))
    return ref[:rows].astype(jnp.float32), jnp.concatenate(spread, axis=0).T


def attend(
    bias, queries, sources, head_size, travels, weight=1
):
    rows, width = queries.shape
    heads = width // head_size
    wide = 2 * head_size
    key_count = sum(source.shape[0] for source in sources)
    block = min(BLOCK, rows)
    if travels:
        held = block + packed_rows(block, width, head_size)
        out_shape = [jax.ShapeDtypeStruct((rows // block * held, width), jnp.bfloat16)]
        out_specs = [pl.BlockSpec((held, width), lambda i: (i, 0))]
    else:
        out_shape = [jax.ShapeDtypeStruct((rows, width), jnp.float32)] * 2
        out_specs = [pl.BlockSpec((block, width), lambda i: (i, 0))] * 2
    return pl.pallas_call(
        partial(attend_kernel, head_size, travels),
        grid=(rows // block,),
        out_shape=out_shape,
        in_specs=[
            pl.BlockSpec(memory_space=VMEM),
            pl.BlockSpec((block, width), lambda i: (i, 0)),
        ]
        + [pl.BlockSpec(memory_space=VMEM)] * len(sources),
        out_specs=out_specs,
        compiler_params=params(),
        cost_estimate=pl.CostEstimate(
            flops=weight * 4 * rows * key_count * wide * heads,
            bytes_accessed=4 * key_count * wide * heads + 8 * rows * wide * heads,
            transcendentals=rows * key_count * heads,
        ),
        name="attend",
    )(bias, queries, *sources)


def merge_kernel(head_size, travels, value_ref, level_ref, *refs):
    parts, out_ref = refs[:-1], refs[-1]
    rows, width = value_ref.shape
    values, levels = [value_ref[...]], [level_ref[...]]
    for ref in parts:
        value, level = unpack(ref, rows, head_size)
        values.append(value)
        levels.append(level)
    top = levels[0]
    for level in levels[1:]:
        top = jnp.maximum(top, level)
    total = jnp.zeros((rows, width), jnp.float32)
    share = jnp.zeros((rows, width), jnp.float32)
    for value, level in zip(values, levels):
        factor = jnp.exp(level - top)
        total = total + value * factor
        share = share + factor
    mixed = total / share
    if travels:
        level = top + jnp.log(share)
        if width < 128:
            level = jnp.concatenate([level, level], axis=1)
        pack(out_ref, mixed, level, head_size)
    else:
        out_ref[...] = mixed.astype(out_ref.dtype)


def merge(value, level, parts, head_size, travels):
    rows, width = value.shape
    held = rows + packed_rows(rows, width, head_size)
    whole = pl.BlockSpec((rows, width), lambda i: (0, 0))
    part_specs = [pl.BlockSpec((held, width), lambda i, k=k: (k, 0)) for _, k in parts]
    out_rows = held if travels else rows
    return pl.pallas_call(
        partial(merge_kernel, head_size, travels),
        grid=(1,),
        out_shape=jax.ShapeDtypeStruct((out_rows, width), jnp.bfloat16),
        in_specs=[whole, whole] + part_specs,
        out_specs=pl.BlockSpec((out_rows, width), lambda i: (0, 0)),
        compiler_params=params(),
        name="merge",
    )(value, level, *[part for part, _ in parts])


def arrange_kernel(place_ref, weight_ref, early_ref, late_ref, semaphores):
    place = place_ref[0]
    count = semaphores.shape[0]
    width = weight_ref.shape[0] // count
    half = count // 2
    copies = []
    for distance in range(count):
        start = pl.multiple_of((place ^ distance) * width, width)
        out_ref = early_ref if distance < half else late_ref
        copy = pltpu.make_async_copy(
            weight_ref.at[pl.ds(start, width)],
            out_ref.at[pl.ds(distance % half * width, width)],
            semaphores.at[distance],
        )
        copy.start()
        copies.append(copy)
    for copy in copies:
        copy.wait()


def arrange(place, out_weight, count):
    depth, columns = out_weight.shape
    return pl.pallas_call(
        arrange_kernel,
        out_shape=[jax.ShapeDtypeStruct((depth // 2, columns), out_weight.dtype)] * 2,
        in_specs=[pl.BlockSpec(memory_space=SMEM), pl.BlockSpec(memory_space=pl.ANY)],
        out_specs=[pl.BlockSpec(memory_space=VMEM)] * 2,
        scratch_shapes=[pltpu.SemaphoreType.DMA((count,))],
        compiler_params=params(),
        name="arrange",
    )(place, out_weight)


def project_early_kernel(weight_ref, *refs):
    blocks, (aged_ref, out_ref, aged_out, semaphore) = refs[:-4], refs[-4:]
    copy = pltpu.make_async_copy(aged_ref, aged_out, semaphore)
    copy.start()
    out_ref[...] = jnp.dot(
        jnp.concatenate([block[...] for block in blocks], axis=1),
        weight_ref[...],
        preferred_element_type=jnp.float32,
    )
    copy.wait()


def project_late_kernel(weight_ref, *refs):
    blocks, (total_ref, out_ref, held, semaphores) = refs[:-4], refs[-4:]
    rows = total_ref.shape[0]
    step = rows // semaphores.shape[0]
    copies = []
    for k in range(semaphores.shape[0]):
        here = slice(k * step, (k + 1) * step)
        total = total_ref[here] + jnp.dot(
            jnp.concatenate([block[here] for block in blocks], axis=1),
            weight_ref[...],
            preferred_element_type=jnp.float32,
        )
        held[here] = total.astype(held.dtype)
        copy = pltpu.make_async_copy(
            held.at[pl.ds(k * step, step)], out_ref.at[pl.ds(k * step, step)], semaphores.at[k]
        )
        copy.start()
        copies.append(copy)
    for copy in copies:
        copy.wait()


def project_cost(rows, columns, depth):
    return pl.CostEstimate(
        flops=2 * rows * columns * depth, bytes_accessed=4 * rows * columns, transcendentals=0
    )


def project_early(out_weight, blocks, aged):
    rows, columns = blocks[0].shape[0], out_weight.shape[1]
    return pl.pallas_call(
        project_early_kernel,
        out_shape=[
            jax.ShapeDtypeStruct((rows, columns), jnp.float32),
            jax.ShapeDtypeStruct(aged.shape, aged.dtype),
        ],
        in_specs=[pl.BlockSpec(memory_space=VMEM)] * (1 + len(blocks))
        + [pl.BlockSpec(memory_space=pl.ANY)],
        out_specs=[pl.BlockSpec(memory_space=VMEM), pl.BlockSpec(memory_space=pl.ANY)],
        scratch_shapes=[pltpu.SemaphoreType.DMA],
        compiler_params=params(),
        cost_estimate=project_cost(rows, columns, blocks[0].shape[1] * len(blocks)),
        name="project_early",
    )(out_weight, *blocks, aged)


def project_late(out_weight, blocks, total):
    rows, columns = total.shape
    return pl.pallas_call(
        project_late_kernel,
        out_shape=jax.ShapeDtypeStruct((rows, columns), jnp.bfloat16),
        in_specs=[pl.BlockSpec(memory_space=VMEM)] * (2 + len(blocks)),
        out_specs=pl.BlockSpec(memory_space=pl.ANY),
        scratch_shapes=[VMEM((rows, columns), jnp.bfloat16), pltpu.SemaphoreType.DMA((4,))],
        compiler_params=params(),
        cost_estimate=project_cost(rows, columns, blocks[0].shape[1] * len(blocks)),
        name="project_late",
    )(out_weight, *blocks, total)


def after(array, *others):
    return lax.optimization_barrier((array, *others))[0]


def gather(mixed, slots, aged):
    half, top = slots // 2, slots - 2
    blocks = {0: mixed, top: exchange(mixed, "slot", top)}
    late = after(mixed, aged)
    blocks[2] = exchange(late, "slot", 2)
    blocks[1] = exchange(late, "slot", 1)
    for d in range(3, half):
        blocks[d] = exchange(late, "slot", d)
    for d in range(1, half):
        blocks[top ^ d] = exchange(blocks[top], "slot", d)
    return blocks


def local(queries, raw_clip, pool_weight, old_memory, valid_columns, out_weight):
    query_rows, model_width = queries.shape
    head_size = model_width // H
    slots = lax.axis_size("slot")
    spaces = lax.axis_size("space")
    columns = old_memory.shape[3]
    width = model_width // slots
    slot_index = lax.axis_index("slot")
    place = slot_index.astype(jnp.int32).reshape(1)
    half = slots // 2

    own_queries = lax.dynamic_slice_in_dim(queries, slot_index * width, width, axis=1)
    evens = range(2, spaces, 2)
    crossed = {e: exchange(own_queries, "space", e) for e in evens}
    near = jnp.concatenate([crossed[e] for e in evens] + [own_queries], axis=0)

    resident = old_memory.reshape(-1, old_memory.shape[-1])
    tokens = resident.shape[0]
    odd_far = tuple(range(half + 1, slots, 2))
    odd_near = tuple(range(1, half, 2))
    far_out, near_out, *kept = cut(
        place, resident, slots, (odd_far, odd_near) + tuple((d,) for d in range(0, slots, 2))
    )
    far_in = exchange(far_out, "slot", 1)
    near_in = exchange(after(near_out, far_in), "slot", 1)
    sources = {0: kept[0], 1: near_in[:tokens]}
    for d in list(range(half, slots, 2))[::-1]:
        row = (d - half) // 2 * tokens
        both = jnp.concatenate([kept[d // 2], far_in[row : row + tokens]], axis=0)
        both = exchange(both, "slot", d)
        sources[d], sources[d + 1] = both[:tokens], both[tokens:]
    below = edge(raw_clip)
    behind = from_behind(below.reshape(-1, below.shape[-1]), "space", 1).reshape(below.shape)
    fresh, fresh_rows = pool(raw_clip, behind, pool_weight, head_size)
    for d in range(2, half, 2):
        row = d // 2 * tokens
        both = jnp.concatenate([kept[d // 2], near_in[row : row + tokens]], axis=0)
        both = exchange(both, "slot", d)
        sources[d], sources[d + 1] = both[:tokens], both[tokens:]
    order = (None,) + tuple(range(slots))
    bias = mask(place, after(valid_columns, fresh_rows), columns, tokens, order)
    far = exchange(after(near, bias), "space", 1)
    aged_memory = from_behind(after(resident, *sources.values(), bias), "slot", 1)
    aged_memory = aged_memory.reshape(old_memory.shape)
    call = partial(
        attend,
        bias,
        sources=[fresh_rows] + [sources[d] for d in range(slots)],
        head_size=head_size,
    )
    parts = []
    for k, e in enumerate(evens):
        rows = slice(k * query_rows, (k + 1) * query_rows)
        (part,) = call(queries=far[rows], travels=True)
        core_part = exchange(part, "space", 1)
        value, level = call(queries=near[rows], travels=False)
        part = merge(value, level, [(core_part, 0)], head_size, True)
        parts.append((exchange(part, "space", e), 0))
        sent_part = part
    (part,) = call(queries=after(far[len(evens) * query_rows :], sent_part), travels=True)
    parts.append((exchange(part, "space", 1), 0))
    value, level = call(queries=own_queries, travels=False, weight=4)
    mixed = merge(value, level, parts, head_size, False)

    blocks = gather(mixed, slots, aged_memory)
    early_weight, late_weight = arrange(place, out_weight, slots)
    total, aged_memory = project_early(early_weight, [blocks[d] for d in range(half)], aged_memory)
    attended = project_late(late_weight, [blocks[d] for d in range(half, slots)], total)
    return (attended, fresh, aged_memory)


def solution(mesh):
    return jax.shard_map(
        local,
        mesh=mesh,
        in_specs=(
            P("space", None),
            P(None, "space", None, "slot"),
            P(None, "slot"),
            P("slot", None, "space", None, None),
            P(),
            P(),
        ),
        out_specs=(
            P("space", None),
            P(None, "space", None, "slot"),
            P("slot", None, "space", None, None),
        ),
        check_vma=False,
    )
```

```python
from functools import partial

import jax
import jax.numpy as jnp
from jax import lax
from jax.experimental import pallas as pl
from jax.experimental.pallas import tpu as pltpu
from jax.sharding import PartitionSpec as P

H = 16
MASKED = -1e30
BLOCK = 512
VMEM_LIMIT = 48 * 1024 * 1024
VMEM = pltpu.VMEM
SMEM = pltpu.SMEM


def params(**more):
    return pltpu.CompilerParams(vmem_limit_bytes=VMEM_LIMIT, **more)


def lanes_of(shape):
    return lax.broadcasted_iota(jnp.int32, shape, len(shape) - 1)


def exchange(block, axis, distance):
    size = lax.axis_size(axis)
    return lax.ppermute(block, axis, [(i, i ^ distance) for i in range(size)])


def from_behind(block, axis, distance):
    devices = range(lax.axis_size(axis))
    return lax.ppermute(block, axis, [(i - distance, i) for i in devices if i - distance in devices])


def pool_kernel(head_size, raw_ref, halo_ref, weight_ref, out_ref, rows_ref, slabs):
    frames, rows, columns, channels = raw_ref.shape
    frames_out, columns_out = frames // 2, columns // 2
    pieces, _, _, wide = slabs.shape
    group = lax.broadcasted_iota(jnp.int32, (wide, wide), 0) // head_size
    averaging = jnp.where(
        group == lanes_of((wide, wide)) // head_size, 1.0 / head_size, 0.0
    ).astype(jnp.float32)
    first_row = lax.broadcasted_iota(jnp.int32, (columns_out, wide), 0) == 0
    mean = partial(
        jnp.dot, precision=lax.Precision.HIGHEST, preferred_element_type=jnp.float32
    )
    for piece in range(pieces):
        lanes = slice(piece * wide, (piece + 1) * wide)
        for f in range(frames):
            slabs[piece, 3 * f] = halo_ref[f, 0, :, lanes].astype(jnp.float32)
            slabs[piece, 3 * f + 1] = raw_ref[f, 0, :, lanes].astype(jnp.float32)
            slabs[piece, 3 * f + 2] = raw_ref[f, 1, :, lanes].astype(jnp.float32)
        weight = weight_ref[:, lanes].astype(jnp.float32)
        for f in range(frames_out):
            sums = [jnp.zeros((columns_out, wide), jnp.float32) for _ in range(3)]
            for a in range(3):
                frame = 2 * f + a - 1
                if frame < 0:
                    continue
                for b in range(3):
                    even = slabs[piece, 3 * frame + b, pl.ds(0, columns_out, stride=2), :]
                    odd = slabs[piece, 3 * frame + b, pl.ds(1, columns_out, stride=2), :]
                    for g, tapped in enumerate((odd, even, odd)):
                        tap = 9 * a + 3 * b + g
                        sums[g] = sums[g] + weight[tap : tap + 1] * tapped
            behind = jnp.where(first_row, 0.0, pltpu.roll(sums[0], 1, 0))
            pooled = behind + sums[1] + sums[2]
            centered = pooled - mean(pooled, averaging)
            spread = mean(centered * centered, averaging)
            normed = (centered * lax.rsqrt(spread + 1e-06)).astype(jnp.bfloat16)
            out_ref[f, 0, :, lanes] = normed
            rows_ref[f * columns_out : (f + 1) * columns_out, lanes] = normed


def edge_kernel(raw_ref, out_ref, semaphore):
    rows = raw_ref.shape[1]
    copy = pltpu.make_async_copy(raw_ref.at[:, pl.ds(rows - 1, 1)], out_ref, semaphore)
    copy.start()
    copy.wait()


def edge(raw_clip):
    frames, rows, columns, channels = raw_clip.shape
    return pl.pallas_call(
        edge_kernel,
        out_shape=jax.ShapeDtypeStruct((frames, 1, columns, channels), raw_clip.dtype),
        in_specs=[pl.BlockSpec(memory_space=pl.ANY)],
        out_specs=pl.BlockSpec(memory_space=VMEM),
        scratch_shapes=[pltpu.SemaphoreType.DMA],
        compiler_params=params(),
        name="edge",
    )(raw_clip)


def pool(raw_clip, halo, pool_weight, head_size):
    frames, rows, columns, channels = raw_clip.shape
    return pl.pallas_call(
        partial(pool_kernel, head_size),
        out_shape=[
            jax.ShapeDtypeStruct((frames // 2, 1, columns // 2, channels), jnp.bfloat16),
            jax.ShapeDtypeStruct((frames // 2 * columns // 2, channels), jnp.bfloat16),
        ],
        in_specs=[pl.BlockSpec(memory_space=VMEM)] * 3,
        out_specs=[pl.BlockSpec(memory_space=VMEM)] * 2,
        scratch_shapes=[VMEM((channels // 128, 3 * frames, columns, 128), jnp.float32)],
        compiler_params=params(),
        name="pool",
    )(raw_clip, halo, pool_weight)


def cut_kernel(width, groups, place_ref, memory_ref, *refs):
    out_refs, semaphores = refs[:-1], refs[-1]
    place = place_ref[0]
    tokens = memory_ref.shape[0]
    copies = []
    for group, out_ref in zip(groups, out_refs):
        for k, distance in enumerate(group):
            start = pl.multiple_of((place ^ distance) * width, 128)
            copy = pltpu.make_async_copy(
                memory_ref.at[:, pl.ds(start, width)],
                out_ref.at[pl.ds(k * tokens, tokens)],
                semaphores.at[len(copies)],
            )
            copy.start()
            copies.append(copy)
    for copy in copies:
        copy.wait()


def cut(place, memory, pieces, groups):
    tokens, channels = memory.shape
    width = channels // pieces
    return pl.pallas_call(
        partial(cut_kernel, width, groups),
        out_shape=[jax.ShapeDtypeStruct((len(g) * tokens, width), memory.dtype) for g in groups],
        in_specs=[pl.BlockSpec(memory_space=SMEM), pl.BlockSpec(memory_space=pl.ANY)],
        out_specs=[pl.BlockSpec(memory_space=VMEM)] * len(groups),
        scratch_shapes=[pltpu.SemaphoreType.DMA((pieces,))],
        compiler_params=params(),
        name="cut",
    )(place, memory)


def mask_kernel(columns, tokens, distances, place_ref, valid_ref, out_ref):
    place = place_ref[0]
    column = lanes_of((out_ref.shape[0], tokens)) % columns
    for k, distance in enumerate(distances):
        valid = valid_ref[0] if distance is None else valid_ref[1 + (place ^ distance)]
        bias = jnp.where(column < valid, 0.0, MASKED)
        out_ref[:, k * tokens : (k + 1) * tokens] = bias


def mask(place, valid, columns, tokens, distances):
    return pl.pallas_call(
        partial(mask_kernel, columns, tokens, distances),
        out_shape=jax.ShapeDtypeStruct((8, tokens * len(distances)), jnp.float32),
        in_specs=[pl.BlockSpec(memory_space=SMEM)] * 2,
        out_specs=pl.BlockSpec(memory_space=VMEM),
        compiler_params=params(),
        name="mask",
    )(place, valid)


def attend_kernel(
    head_size, travels, bias_ref, query_ref, *refs
):
    outs = 1 if travels else 2
    sources, out_refs = refs[:-outs], refs[-outs:]
    rows, width = query_ref.shape
    heads = width // head_size
    wide = 2 * head_size
    lane = lanes_of((rows, wide))
    queries = query_ref[...].astype(jnp.float32) * head_size ** (-0.5)
    groups = [sources[: len(sources) // 2 + 1], sources[len(sources) // 2 + 1 :]]
    memory, scores = [], []
    for h in range(heads):
        own = queries if h == 0 else pltpu.roll(queries, width - h * head_size, 1)
        if own.shape[1] < wide:
            own = jnp.concatenate([own, own], axis=1)
        own = jnp.where(lane < head_size, own, 0.0).astype(jnp.bfloat16)
        memory.append([])
        scores.append([])
        at = 0
        for group in groups:
            held = [source[:, h * wide : (h + 1) * wide] for source in group]
            memory[h].append(jnp.concatenate(held, axis=0))
            product = lax.dot_general(
                own, memory[h][-1], (((1,), (1,)), ((), ())), preferred_element_type=jnp.float32
            )
            count = product.shape[1]
            scores[h].append(product + bias_ref[:1, at : at + count])
            at += count
    weights, peaks = [], []
    for h in range(heads):
        peak = jnp.max(scores[h][0], axis=1, keepdims=True)
        for part in scores[h][1:]:
            peak = jnp.maximum(peak, jnp.max(part, axis=1, keepdims=True))
        peaks.append(peak)
        weights.append([jnp.exp(part - peak).astype(jnp.bfloat16) for part in scores[h]])
    totals = []
    for h in range(heads):
        total = None
        for held, weight in zip(memory[h], weights[h]):
            ones_and_values = jnp.where(lanes_of(held.shape) < head_size, 1.0, held.astype(jnp.float32))
            term = jnp.dot(
                weight, ones_and_values.astype(jnp.bfloat16), preferred_element_type=jnp.float32
            )
            total = term if total is None else total + term
        totals.append(total)
    if heads == 1:
        turned = pltpu.roll(totals[0], head_size, 1)
        value = (turned / totals[0])[:, :head_size]
        level = jnp.log(totals[0]) + peaks[0]
    else:
        first = lane < head_size
        sums = jnp.where(first, totals[0], pltpu.roll(totals[1], head_size, 1))
        value = jnp.where(first, pltpu.roll(totals[0], head_size, 1), totals[1]) / sums
        level = jnp.log(sums) + jnp.where(first, peaks[0], peaks[1])
    if travels:
        pack(out_refs[0], value, level, head_size)
    else:
        out_refs[0][...] = value
        out_refs[1][...] = level[:, :width]


def packed_rows(rows, width, head_size):
    return -(-3 * (width // head_size) * rows // width // 16) * 16


def pack(out_ref, value, level, head_size):
    rows, width = value.shape
    out_ref[:rows] = value.astype(out_ref.dtype)
    turned = level.T
    lines = []
    for h in range(width // head_size):
        rest = turned[h * head_size : h * head_size + 1, :]
        for _ in range(3):
            term = rest.astype(jnp.bfloat16).astype(jnp.float32)
            rest = rest - term
            lines += [term[:, j : j + width] for j in range(0, rows, width)]
    below = packed_rows(rows, width, head_size)
    if len(lines) < below:
        lines.append(jnp.zeros((below - len(lines), width), jnp.float32))
    out_ref[rows:] = jnp.concatenate(lines, axis=0).astype(out_ref.dtype)


def unpack(ref, rows, head_size):
    width = ref.shape[1]
    packed = ref[rows:].astype(jnp.float32)
    count = rows // width
    spread = []
    for h in range(width // head_size):
        first = 3 * h * count
        line = [
            packed[j : j + 1] + packed[j + count : j + count + 1] + packed[j + 2 * count : j + 2 * count + 1]
            for j in range(first, first + count)
        ]
        spread.append(jnp.broadcast_to(jnp.concatenate(line, axis=1), (head_size, rows)))
    return ref[:rows].astype(jnp.float32), jnp.concatenate(spread, axis=0).T


def attend(
    bias, queries, sources, head_size, travels, weight=1
):
    rows, width = queries.shape
    heads = width // head_size
    wide = 2 * head_size
    key_count = sum(source.shape[0] for source in sources)
    block = min(BLOCK, rows)
    if travels:
        held = block + packed_rows(block, width, head_size)
        out_shape = [jax.ShapeDtypeStruct((rows // block * held, width), jnp.bfloat16)]
        out_specs = [pl.BlockSpec((held, width), lambda i: (i, 0))]
    else:
        out_shape = [jax.ShapeDtypeStruct((rows, width), jnp.float32)] * 2
        out_specs = [pl.BlockSpec((block, width), lambda i: (i, 0))] * 2
    return pl.pallas_call(
        partial(attend_kernel, head_size, travels),
        grid=(rows // block,),
        out_shape=out_shape,
        in_specs=[
            pl.BlockSpec(memory_space=VMEM),
            pl.BlockSpec((block, width), lambda i: (i, 0)),
        ]
        + [pl.BlockSpec(memory_space=VMEM)] * len(sources),
        out_specs=out_specs,
        compiler_params=params(),
        cost_estimate=pl.CostEstimate(
            flops=weight * 4 * rows * key_count * wide * heads,
            bytes_accessed=4 * key_count * wide * heads + 8 * rows * wide * heads,
            transcendentals=rows * key_count * heads,
        ),
        name="attend",
    )(bias, queries, *sources)


def merge_kernel(head_size, travels, value_ref, level_ref, *refs):
    parts, out_ref = refs[:-1], refs[-1]
    rows, width = value_ref.shape
    values, levels = [value_ref[...]], [level_ref[...]]
    for ref in parts:
        value, level = unpack(ref, rows, head_size)
        values.append(value)
        levels.append(level)
    top = levels[0]
    for level in levels[1:]:
        top = jnp.maximum(top, level)
    total = jnp.zeros((rows, width), jnp.float32)
    share = jnp.zeros((rows, width), jnp.float32)
    for value, level in zip(values, levels):
        factor = jnp.exp(level - top)
        total = total + value * factor
        share = share + factor
    mixed = total / share
    if travels:
        level = top + jnp.log(share)
        if width < 128:
            level = jnp.concatenate([level, level], axis=1)
        pack(out_ref, mixed, level, head_size)
    else:
        out_ref[...] = mixed.astype(out_ref.dtype)


def merge(value, level, parts, head_size, travels):
    rows, width = value.shape
    held = rows + packed_rows(rows, width, head_size)
    whole = pl.BlockSpec((rows, width), lambda i: (0, 0))
    part_specs = [pl.BlockSpec((held, width), lambda i, k=k: (k, 0)) for _, k in parts]
    out_rows = held if travels else rows
    return pl.pallas_call(
        partial(merge_kernel, head_size, travels),
        grid=(1,),
        out_shape=jax.ShapeDtypeStruct((out_rows, width), jnp.bfloat16),
        in_specs=[whole, whole] + part_specs,
        out_specs=pl.BlockSpec((out_rows, width), lambda i: (0, 0)),
        compiler_params=params(),
        name="merge",
    )(value, level, *[part for part, _ in parts])


def arrange_kernel(place_ref, weight_ref, early_ref, late_ref, semaphores):
    place = place_ref[0]
    count = semaphores.shape[0]
    width = weight_ref.shape[0] // count
    half = count // 2
    copies = []
    for distance in range(count):
        start = pl.multiple_of((place ^ distance) * width, width)
        out_ref = early_ref if distance < half else late_ref
        copy = pltpu.make_async_copy(
            weight_ref.at[pl.ds(start, width)],
            out_ref.at[pl.ds(distance % half * width, width)],
            semaphores.at[distance],
        )
        copy.start()
        copies.append(copy)
    for copy in copies:
        copy.wait()


def arrange(place, out_weight, count):
    depth, columns = out_weight.shape
    return pl.pallas_call(
        arrange_kernel,
        out_shape=[jax.ShapeDtypeStruct((depth // 2, columns), out_weight.dtype)] * 2,
        in_specs=[pl.BlockSpec(memory_space=SMEM), pl.BlockSpec(memory_space=pl.ANY)],
        out_specs=[pl.BlockSpec(memory_space=VMEM)] * 2,
        scratch_shapes=[pltpu.SemaphoreType.DMA((count,))],
        compiler_params=params(),
        name="arrange",
    )(place, out_weight)


def project_early_kernel(weight_ref, *refs):
    blocks, (aged_ref, out_ref, aged_out, semaphore) = refs[:-4], refs[-4:]
    copy = pltpu.make_async_copy(aged_ref, aged_out, semaphore)
    copy.start()
    out_ref[...] = jnp.dot(
        jnp.concatenate([block[...] for block in blocks], axis=1),
        weight_ref[...],
        preferred_element_type=jnp.float32,
    )
    copy.wait()


def project_late_kernel(weight_ref, *refs):
    blocks, (total_ref, out_ref, held, semaphores) = refs[:-4], refs[-4:]
    rows = total_ref.shape[0]
    step = rows // semaphores.shape[0]
    copies = []
    for k in range(semaphores.shape[0]):
        here = slice(k * step, (k + 1) * step)
        total = total_ref[here] + jnp.dot(
            jnp.concatenate([block[here] for block in blocks], axis=1),
            weight_ref[...],
            preferred_element_type=jnp.float32,
        )
        held[here] = total.astype(held.dtype)
        copy = pltpu.make_async_copy(
            held.at[pl.ds(k * step, step)], out_ref.at[pl.ds(k * step, step)], semaphores.at[k]
        )
        copy.start()
        copies.append(copy)
    for copy in copies:
        copy.wait()


def project_cost(rows, columns, depth):
    return pl.CostEstimate(
        flops=2 * rows * columns * depth, bytes_accessed=4 * rows * columns, transcendentals=0
    )


def project_early(out_weight, blocks, aged):
    rows, columns = blocks[0].shape[0], out_weight.shape[1]
    return pl.pallas_call(
        project_early_kernel,
        out_shape=[
            jax.ShapeDtypeStruct((rows, columns), jnp.float32),
            jax.ShapeDtypeStruct(aged.shape, aged.dtype),
        ],
        in_specs=[pl.BlockSpec(memory_space=VMEM)] * (1 + len(blocks))
        + [pl.BlockSpec(memory_space=pl.ANY)],
        out_specs=[pl.BlockSpec(memory_space=VMEM), pl.BlockSpec(memory_space=pl.ANY)],
        scratch_shapes=[pltpu.SemaphoreType.DMA],
        compiler_params=params(),
        cost_estimate=project_cost(rows, columns, blocks[0].shape[1] * len(blocks)),
        name="project_early",
    )(out_weight, *blocks, aged)


def project_late(out_weight, blocks, total):
    rows, columns = total.shape
    return pl.pallas_call(
        project_late_kernel,
        out_shape=jax.ShapeDtypeStruct((rows, columns), jnp.bfloat16),
        in_specs=[pl.BlockSpec(memory_space=VMEM)] * (2 + len(blocks)),
        out_specs=pl.BlockSpec(memory_space=pl.ANY),
        scratch_shapes=[VMEM((rows, columns), jnp.bfloat16), pltpu.SemaphoreType.DMA((4,))],
        compiler_params=params(),
        cost_estimate=project_cost(rows, columns, blocks[0].shape[1] * len(blocks)),
        name="project_late",
    )(out_weight, *blocks, total)


def after(array, *others):
    return lax.optimization_barrier((array, *others))[0]


def gather(mixed, slots, aged):
    half, top = slots // 2, slots - 2
    blocks = {0: mixed, top: exchange(mixed, "slot", top)}
    late = after(mixed, *aged)
    blocks[2] = exchange(late, "slot", 2)
    blocks[1] = exchange(late, "slot", 1)
    for d in range(3, half):
        blocks[d] = exchange(late, "slot", d)
    for d in range(1, half):
        blocks[top ^ d] = exchange(blocks[top], "slot", d)
    return blocks


def local(queries, raw_clip, pool_weight, old_memory, valid_columns, out_weight):
    query_rows, model_width = queries.shape
    head_size = model_width // H
    slots = lax.axis_size("slot")
    spaces = lax.axis_size("space")
    columns = old_memory.shape[3]
    width = model_width // slots
    slot_index = lax.axis_index("slot")
    place = slot_index.astype(jnp.int32).reshape(1)
    half = slots // 2

    own_queries = lax.dynamic_slice_in_dim(queries, slot_index * width, width, axis=1)
    evens = range(2, spaces, 2)
    crossed = {e: exchange(own_queries, "space", e) for e in evens}
    near = jnp.concatenate([crossed[e] for e in evens] + [own_queries], axis=0)

    resident = old_memory.reshape(-1, old_memory.shape[-1])
    tokens = resident.shape[0]
    odd_far = tuple(range(half + 1, slots, 2))
    odd_near = tuple(range(1, half, 2))
    far_out, near_out, *kept = cut(
        place, resident, slots, (odd_far, odd_near) + tuple((d,) for d in range(0, slots, 2))
    )
    far_in = exchange(far_out, "slot", 1)
    near_in = exchange(after(near_out, far_in), "slot", 1)
    sources = {0: kept[0], 1: near_in[:tokens]}
    for d in list(range(half, slots, 2))[::-1]:
        row = (d - half) // 2 * tokens
        both = jnp.concatenate([kept[d // 2], far_in[row : row + tokens]], axis=0)
        both = exchange(both, "slot", d)
        sources[d], sources[d + 1] = both[:tokens], both[tokens:]
    below = edge(raw_clip)
    behind = from_behind(below.reshape(-1, below.shape[-1]), "space", 1).reshape(below.shape)
    fresh, fresh_rows = pool(raw_clip, behind, pool_weight, head_size)
    for d in range(2, half, 2):
        row = d // 2 * tokens
        both = jnp.concatenate([kept[d // 2], near_in[row : row + tokens]], axis=0)
        both = exchange(both, "slot", d)
        sources[d], sources[d + 1] = both[:tokens], both[tokens:]
    order = (None,) + tuple(range(slots))
    bias = mask(place, after(valid_columns, fresh_rows), columns, tokens, order)
    far = exchange(after(near, bias), "space", 1)
    inside = [(i, i + 1) for i in range(0, slots, 2)]
    onward = [(i, i + 1) for i in range(1, slots - 1, 2)]
    inside = lax.ppermute(after(resident, near_in), "slot", inside)
    onward = lax.ppermute(after(resident, *sources.values(), bias), "slot", onward)
    call = partial(
        attend,
        bias,
        sources=[fresh_rows] + [sources[d] for d in range(slots)],
        head_size=head_size,
    )
    parts = []
    for k, e in enumerate(evens):
        rows = slice(k * query_rows, (k + 1) * query_rows)
        (part,) = call(queries=far[rows], travels=True)
        core_part = exchange(part, "space", 1)
        value, level = call(queries=near[rows], travels=False)
        part = merge(value, level, [(core_part, 0)], head_size, True)
        parts.append((exchange(part, "space", e), 0))
        sent_part = part
    (part,) = call(queries=after(far[len(evens) * query_rows :], sent_part), travels=True)
    parts.append((exchange(part, "space", 1), 0))
    value, level = call(queries=own_queries, travels=False, weight=4)
    mixed = merge(value, level, parts, head_size, False)

    blocks = gather(mixed, slots, (inside, onward))
    aged_memory = jnp.where(slot_index % 2 == 1, inside, onward).reshape(old_memory.shape)
    early_weight, late_weight = arrange(place, out_weight, slots)
    total, aged_memory = project_early(early_weight, [blocks[d] for d in range(half)], aged_memory)
    attended = project_late(late_weight, [blocks[d] for d in range(half, slots)], total)
    return (attended, fresh, aged_memory)


def solution(mesh):
    return jax.shard_map(
        local,
        mesh=mesh,
        in_specs=(
            P("space", None),
            P(None, "space", None, "slot"),
            P(None, "slot"),
            P("slot", None, "space", None, None),
            P(),
            P(),
        ),
        out_specs=(
            P("space", None),
            P(None, "space", None, "slot"),
            P("slot", None, "space", None, None),
        ),
        check_vma=False,
    )
```

```python
from functools import partial

import jax
import jax.numpy as jnp
from jax import lax
from jax.experimental import pallas as pl
from jax.experimental.pallas import tpu as pltpu
from jax.sharding import PartitionSpec as P

H = 16
MASKED = -1e30
BLOCK = 512
VMEM_LIMIT = 48 * 1024 * 1024
VMEM = pltpu.VMEM
SMEM = pltpu.SMEM


def params(**more):
    return pltpu.CompilerParams(vmem_limit_bytes=VMEM_LIMIT, **more)


def lanes_of(shape):
    return lax.broadcasted_iota(jnp.int32, shape, len(shape) - 1)


def exchange(block, axis, distance):
    size = lax.axis_size(axis)
    return lax.ppermute(block, axis, [(i, i ^ distance) for i in range(size)])


def from_behind(block, axis, distance):
    devices = range(lax.axis_size(axis))
    return lax.ppermute(block, axis, [(i - distance, i) for i in devices if i - distance in devices])


def pool_kernel(head_size, raw_ref, halo_ref, weight_ref, out_ref, rows_ref, slabs):
    frames, rows, columns, channels = raw_ref.shape
    frames_out, columns_out = frames // 2, columns // 2
    pieces, _, _, wide = slabs.shape
    group = lax.broadcasted_iota(jnp.int32, (wide, wide), 0) // head_size
    averaging = jnp.where(
        group == lanes_of((wide, wide)) // head_size, 1.0 / head_size, 0.0
    ).astype(jnp.float32)
    first_row = lax.broadcasted_iota(jnp.int32, (columns_out, wide), 0) == 0
    mean = partial(
        jnp.dot, precision=lax.Precision.HIGHEST, preferred_element_type=jnp.float32
    )
    for piece in range(pieces):
        lanes = slice(piece * wide, (piece + 1) * wide)
        for f in range(frames):
            slabs[piece, 3 * f] = halo_ref[f, 0, :, lanes].astype(jnp.float32)
            slabs[piece, 3 * f + 1] = raw_ref[f, 0, :, lanes].astype(jnp.float32)
            slabs[piece, 3 * f + 2] = raw_ref[f, 1, :, lanes].astype(jnp.float32)
        weight = weight_ref[:, lanes].astype(jnp.float32)
        for f in range(frames_out):
            sums = [jnp.zeros((columns_out, wide), jnp.float32) for _ in range(3)]
            for a in range(3):
                frame = 2 * f + a - 1
                if frame < 0:
                    continue
                for b in range(3):
                    even = slabs[piece, 3 * frame + b, pl.ds(0, columns_out, stride=2), :]
                    odd = slabs[piece, 3 * frame + b, pl.ds(1, columns_out, stride=2), :]
                    for g, tapped in enumerate((odd, even, odd)):
                        tap = 9 * a + 3 * b + g
                        sums[g] = sums[g] + weight[tap : tap + 1] * tapped
            behind = jnp.where(first_row, 0.0, pltpu.roll(sums[0], 1, 0))
            pooled = behind + sums[1] + sums[2]
            centered = pooled - mean(pooled, averaging)
            spread = mean(centered * centered, averaging)
            normed = (centered * lax.rsqrt(spread + 1e-06)).astype(jnp.bfloat16)
            out_ref[f, 0, :, lanes] = normed
            rows_ref[f * columns_out : (f + 1) * columns_out, lanes] = normed


def edge_kernel(raw_ref, out_ref, semaphore):
    rows = raw_ref.shape[1]
    copy = pltpu.make_async_copy(raw_ref.at[:, pl.ds(rows - 1, 1)], out_ref, semaphore)
    copy.start()
    copy.wait()


def edge(raw_clip):
    frames, rows, columns, channels = raw_clip.shape
    return pl.pallas_call(
        edge_kernel,
        out_shape=jax.ShapeDtypeStruct((frames, 1, columns, channels), raw_clip.dtype),
        in_specs=[pl.BlockSpec(memory_space=pl.ANY)],
        out_specs=pl.BlockSpec(memory_space=VMEM),
        scratch_shapes=[pltpu.SemaphoreType.DMA],
        compiler_params=params(),
        name="edge",
    )(raw_clip)


def pool(raw_clip, halo, pool_weight, head_size):
    frames, rows, columns, channels = raw_clip.shape
    return pl.pallas_call(
        partial(pool_kernel, head_size),
        out_shape=[
            jax.ShapeDtypeStruct((frames // 2, 1, columns // 2, channels), jnp.bfloat16),
            jax.ShapeDtypeStruct((frames // 2 * columns // 2, channels), jnp.bfloat16),
        ],
        in_specs=[pl.BlockSpec(memory_space=VMEM)] * 3,
        out_specs=[pl.BlockSpec(memory_space=VMEM)] * 2,
        scratch_shapes=[VMEM((channels // 128, 3 * frames, columns, 128), jnp.float32)],
        compiler_params=params(),
        name="pool",
    )(raw_clip, halo, pool_weight)


def cut_kernel(width, groups, place_ref, memory_ref, *refs):
    out_refs, semaphores = refs[:-1], refs[-1]
    place = place_ref[0]
    tokens = memory_ref.shape[0]
    copies = []
    for group, out_ref in zip(groups, out_refs):
        for k, distance in enumerate(group):
            start = pl.multiple_of((place ^ distance) * width, 128)
            copy = pltpu.make_async_copy(
                memory_ref.at[:, pl.ds(start, width)],
                out_ref.at[pl.ds(k * tokens, tokens)],
                semaphores.at[len(copies)],
            )
            copy.start()
            copies.append(copy)
    for copy in copies:
        copy.wait()


def cut(place, memory, pieces, groups):
    tokens, channels = memory.shape
    width = channels // pieces
    return pl.pallas_call(
        partial(cut_kernel, width, groups),
        out_shape=[jax.ShapeDtypeStruct((len(g) * tokens, width), memory.dtype) for g in groups],
        in_specs=[pl.BlockSpec(memory_space=SMEM), pl.BlockSpec(memory_space=pl.ANY)],
        out_specs=[pl.BlockSpec(memory_space=VMEM)] * len(groups),
        scratch_shapes=[pltpu.SemaphoreType.DMA((pieces,))],
        compiler_params=params(),
        name="cut",
    )(place, memory)


def mask_kernel(columns, tokens, distances, place_ref, valid_ref, out_ref):
    place = place_ref[0]
    column = lanes_of((out_ref.shape[0], tokens)) % columns
    for k, distance in enumerate(distances):
        valid = valid_ref[0] if distance is None else valid_ref[1 + (place ^ distance)]
        bias = jnp.where(column < valid, 0.0, MASKED)
        out_ref[:, k * tokens : (k + 1) * tokens] = bias


def mask(place, valid, columns, tokens, distances):
    return pl.pallas_call(
        partial(mask_kernel, columns, tokens, distances),
        out_shape=jax.ShapeDtypeStruct((8, tokens * len(distances)), jnp.float32),
        in_specs=[pl.BlockSpec(memory_space=SMEM)] * 2,
        out_specs=pl.BlockSpec(memory_space=VMEM),
        compiler_params=params(),
        name="mask",
    )(place, valid)


def attend_kernel(
    head_size, travels, bias_ref, query_ref, *refs
):
    outs = 1 if travels else 2
    sources, out_refs = refs[:-outs], refs[-outs:]
    rows, width = query_ref.shape
    heads = width // head_size
    wide = 2 * head_size
    lane = lanes_of((rows, wide))
    queries = query_ref[...].astype(jnp.float32) * head_size ** (-0.5)
    groups = [sources[: len(sources) // 2 + 1], sources[len(sources) // 2 + 1 :]]
    memory, scores = [], []
    for h in range(heads):
        own = queries if h == 0 else pltpu.roll(queries, width - h * head_size, 1)
        if own.shape[1] < wide:
            own = jnp.concatenate([own, own], axis=1)
        own = jnp.where(lane < head_size, own, 0.0).astype(jnp.bfloat16)
        memory.append([])
        scores.append([])
        at = 0
        for group in groups:
            held = [source[:, h * wide : (h + 1) * wide] for source in group]
            memory[h].append(jnp.concatenate(held, axis=0))
            product = lax.dot_general(
                own, memory[h][-1], (((1,), (1,)), ((), ())), preferred_element_type=jnp.float32
            )
            count = product.shape[1]
            scores[h].append(product + bias_ref[:1, at : at + count])
            at += count
    weights, peaks = [], []
    for h in range(heads):
        peak = jnp.max(scores[h][0], axis=1, keepdims=True)
        for part in scores[h][1:]:
            peak = jnp.maximum(peak, jnp.max(part, axis=1, keepdims=True))
        peaks.append(peak)
        weights.append([jnp.exp(part - peak).astype(jnp.bfloat16) for part in scores[h]])
    totals = []
    for h in range(heads):
        total = None
        for held, weight in zip(memory[h], weights[h]):
            ones_and_values = jnp.where(lanes_of(held.shape) < head_size, 1.0, held.astype(jnp.float32))
            term = jnp.dot(
                weight, ones_and_values.astype(jnp.bfloat16), preferred_element_type=jnp.float32
            )
            total = term if total is None else total + term
        totals.append(total)
    if heads == 1:
        turned = pltpu.roll(totals[0], head_size, 1)
        value = (turned / totals[0])[:, :head_size]
        level = jnp.log(totals[0]) + peaks[0]
    else:
        first = lane < head_size
        sums = jnp.where(first, totals[0], pltpu.roll(totals[1], head_size, 1))
        value = jnp.where(first, pltpu.roll(totals[0], head_size, 1), totals[1]) / sums
        level = jnp.log(sums) + jnp.where(first, peaks[0], peaks[1])
    if travels:
        pack(out_refs[0], value, level, head_size)
    else:
        out_refs[0][...] = value
        out_refs[1][...] = level[:, :width]


def packed_rows(rows, width, head_size):
    return -(-3 * (width // head_size) * rows // width // 16) * 16


def pack(out_ref, value, level, head_size):
    rows, width = value.shape
    out_ref[:rows] = value.astype(out_ref.dtype)
    turned = level.T
    lines = []
    for h in range(width // head_size):
        rest = turned[h * head_size : h * head_size + 1, :]
        for _ in range(3):
            term = rest.astype(jnp.bfloat16).astype(jnp.float32)
            rest = rest - term
            lines += [term[:, j : j + width] for j in range(0, rows, width)]
    below = packed_rows(rows, width, head_size)
    if len(lines) < below:
        lines.append(jnp.zeros((below - len(lines), width), jnp.float32))
    out_ref[rows:] = jnp.concatenate(lines, axis=0).astype(out_ref.dtype)


def unpack(ref, rows, head_size):
    width = ref.shape[1]
    packed = ref[rows:].astype(jnp.float32)
    count = rows // width
    spread = []
    for h in range(width // head_size):
        first = 3 * h * count
        line = [
            packed[j : j + 1] + packed[j + count : j + count + 1] + packed[j + 2 * count : j + 2 * count + 1]
            for j in range(first, first + count)
        ]
        spread.append(jnp.broadcast_to(jnp.concatenate(line, axis=1), (head_size, rows)))
    return ref[:rows].astype(jnp.float32), jnp.concatenate(spread, axis=0).T


def attend(
    bias, queries, sources, head_size, travels, weight=1
):
    rows, width = queries.shape
    heads = width // head_size
    wide = 2 * head_size
    key_count = sum(source.shape[0] for source in sources)
    block = min(BLOCK, rows)
    if travels:
        held = block + packed_rows(block, width, head_size)
        out_shape = [jax.ShapeDtypeStruct((rows // block * held, width), jnp.bfloat16)]
        out_specs = [pl.BlockSpec((held, width), lambda i: (i, 0))]
    else:
        out_shape = [jax.ShapeDtypeStruct((rows, width), jnp.float32)] * 2
        out_specs = [pl.BlockSpec((block, width), lambda i: (i, 0))] * 2
    return pl.pallas_call(
        partial(attend_kernel, head_size, travels),
        grid=(rows // block,),
        out_shape=out_shape,
        in_specs=[
            pl.BlockSpec(memory_space=VMEM),
            pl.BlockSpec((block, width), lambda i: (i, 0)),
        ]
        + [pl.BlockSpec(memory_space=VMEM)] * len(sources),
        out_specs=out_specs,
        compiler_params=params(),
        cost_estimate=pl.CostEstimate(
            flops=weight * 4 * rows * key_count * wide * heads,
            bytes_accessed=4 * key_count * wide * heads + 8 * rows * wide * heads,
            transcendentals=rows * key_count * heads,
        ),
        name="attend",
    )(bias, queries, *sources)


def merge_kernel(head_size, travels, value_ref, level_ref, *refs):
    parts, out_ref = refs[:-1], refs[-1]
    rows, width = value_ref.shape
    values, levels = [value_ref[...]], [level_ref[...]]
    for ref in parts:
        value, level = unpack(ref, rows, head_size)
        values.append(value)
        levels.append(level)
    top = levels[0]
    for level in levels[1:]:
        top = jnp.maximum(top, level)
    total = jnp.zeros((rows, width), jnp.float32)
    share = jnp.zeros((rows, width), jnp.float32)
    for value, level in zip(values, levels):
        factor = jnp.exp(level - top)
        total = total + value * factor
        share = share + factor
    mixed = total / share
    if travels:
        level = top + jnp.log(share)
        if width < 128:
            level = jnp.concatenate([level, level], axis=1)
        pack(out_ref, mixed, level, head_size)
    else:
        out_ref[...] = mixed.astype(out_ref.dtype)


def merge(value, level, parts, head_size, travels):
    rows, width = value.shape
    held = rows + packed_rows(rows, width, head_size)
    whole = pl.BlockSpec((rows, width), lambda i: (0, 0))
    part_specs = [pl.BlockSpec((held, width), lambda i, k=k: (k, 0)) for _, k in parts]
    out_rows = held if travels else rows
    return pl.pallas_call(
        partial(merge_kernel, head_size, travels),
        grid=(1,),
        out_shape=jax.ShapeDtypeStruct((out_rows, width), jnp.bfloat16),
        in_specs=[whole, whole] + part_specs,
        out_specs=pl.BlockSpec((out_rows, width), lambda i: (0, 0)),
        compiler_params=params(),
        name="merge",
    )(value, level, *[part for part, _ in parts])


def arrange_kernel(place_ref, weight_ref, early_ref, late_ref, semaphores):
    place = place_ref[0]
    count = semaphores.shape[0]
    width = weight_ref.shape[0] // count
    half = count // 2
    copies = []
    for distance in range(count):
        start = pl.multiple_of((place ^ distance) * width, width)
        out_ref = early_ref if distance < half else late_ref
        copy = pltpu.make_async_copy(
            weight_ref.at[pl.ds(start, width)],
            out_ref.at[pl.ds(distance % half * width, width)],
            semaphores.at[distance],
        )
        copy.start()
        copies.append(copy)
    for copy in copies:
        copy.wait()


def arrange(place, out_weight, count):
    depth, columns = out_weight.shape
    return pl.pallas_call(
        arrange_kernel,
        out_shape=[jax.ShapeDtypeStruct((depth // 2, columns), out_weight.dtype)] * 2,
        in_specs=[pl.BlockSpec(memory_space=SMEM), pl.BlockSpec(memory_space=pl.ANY)],
        out_specs=[pl.BlockSpec(memory_space=VMEM)] * 2,
        scratch_shapes=[pltpu.SemaphoreType.DMA((count,))],
        compiler_params=params(),
        name="arrange",
    )(place, out_weight)


def project_early_kernel(weight_ref, *refs):
    blocks, (aged_ref, out_ref, aged_out, semaphore) = refs[:-4], refs[-4:]
    copy = pltpu.make_async_copy(aged_ref, aged_out, semaphore)
    copy.start()
    out_ref[...] = jnp.dot(
        jnp.concatenate([block[...] for block in blocks], axis=1),
        weight_ref[...],
        preferred_element_type=jnp.float32,
    )
    copy.wait()


def project_late_kernel(weight_ref, *refs):
    blocks, (total_ref, out_ref, held, semaphores) = refs[:-4], refs[-4:]
    rows = total_ref.shape[0]
    step = rows // semaphores.shape[0]
    copies = []
    for k in range(semaphores.shape[0]):
        here = slice(k * step, (k + 1) * step)
        total = total_ref[here] + jnp.dot(
            jnp.concatenate([block[here] for block in blocks], axis=1),
            weight_ref[...],
            preferred_element_type=jnp.float32,
        )
        held[here] = total.astype(held.dtype)
        copy = pltpu.make_async_copy(
            held.at[pl.ds(k * step, step)], out_ref.at[pl.ds(k * step, step)], semaphores.at[k]
        )
        copy.start()
        copies.append(copy)
    for copy in copies:
        copy.wait()


def project_cost(rows, columns, depth):
    return pl.CostEstimate(
        flops=2 * rows * columns * depth, bytes_accessed=4 * rows * columns, transcendentals=0
    )


def project_early(out_weight, blocks, aged):
    rows, columns = blocks[0].shape[0], out_weight.shape[1]
    return pl.pallas_call(
        project_early_kernel,
        out_shape=[
            jax.ShapeDtypeStruct((rows, columns), jnp.float32),
            jax.ShapeDtypeStruct(aged.shape, aged.dtype),
        ],
        in_specs=[pl.BlockSpec(memory_space=VMEM)] * (1 + len(blocks))
        + [pl.BlockSpec(memory_space=pl.ANY)],
        out_specs=[pl.BlockSpec(memory_space=VMEM), pl.BlockSpec(memory_space=pl.ANY)],
        scratch_shapes=[pltpu.SemaphoreType.DMA],
        compiler_params=params(),
        cost_estimate=project_cost(rows, columns, blocks[0].shape[1] * len(blocks)),
        name="project_early",
    )(out_weight, *blocks, aged)


def project_late(out_weight, blocks, total):
    rows, columns = total.shape
    return pl.pallas_call(
        project_late_kernel,
        out_shape=jax.ShapeDtypeStruct((rows, columns), jnp.bfloat16),
        in_specs=[pl.BlockSpec(memory_space=VMEM)] * (2 + len(blocks)),
        out_specs=pl.BlockSpec(memory_space=pl.ANY),
        scratch_shapes=[VMEM((rows, columns), jnp.bfloat16), pltpu.SemaphoreType.DMA((4,))],
        compiler_params=params(),
        cost_estimate=project_cost(rows, columns, blocks[0].shape[1] * len(blocks)),
        name="project_late",
    )(out_weight, *blocks, total)


def after(array, *others):
    return lax.optimization_barrier((array, *others))[0]


def gather(mixed, slots, aged):
    half, top = slots // 2, slots - 2
    blocks = {0: mixed, top: exchange(mixed, "slot", top)}
    late = after(mixed, *aged)
    blocks[2] = exchange(late, "slot", 2)
    blocks[1] = exchange(mixed, "slot", 1)
    for d in range(3, half):
        blocks[d] = exchange(late, "slot", d)
    for d in range(1, half):
        blocks[top ^ d] = exchange(blocks[top], "slot", d)
    return blocks


def local(queries, raw_clip, pool_weight, old_memory, valid_columns, out_weight):
    query_rows, model_width = queries.shape
    head_size = model_width // H
    slots = lax.axis_size("slot")
    spaces = lax.axis_size("space")
    columns = old_memory.shape[3]
    width = model_width // slots
    slot_index = lax.axis_index("slot")
    place = slot_index.astype(jnp.int32).reshape(1)
    half = slots // 2

    own_queries = lax.dynamic_slice_in_dim(queries, slot_index * width, width, axis=1)
    evens = range(2, spaces, 2)
    crossed = {e: exchange(own_queries, "space", e) for e in evens}
    near = jnp.concatenate([crossed[e] for e in evens] + [own_queries], axis=0)

    resident = old_memory.reshape(-1, old_memory.shape[-1])
    tokens = resident.shape[0]
    odd_far = tuple(range(half + 1, slots, 2))
    odd_near = tuple(range(1, half, 2))
    far_out, near_out, *kept = cut(
        place, resident, slots, (odd_far, odd_near) + tuple((d,) for d in range(0, slots, 2))
    )
    far_in = exchange(far_out, "slot", 1)
    near_in = exchange(after(near_out, far_in), "slot", 1)
    sources = {0: kept[0], 1: near_in[:tokens]}
    for d in list(range(half, slots, 2))[::-1]:
        row = (d - half) // 2 * tokens
        both = jnp.concatenate([kept[d // 2], far_in[row : row + tokens]], axis=0)
        both = exchange(both, "slot", d)
        sources[d], sources[d + 1] = both[:tokens], both[tokens:]
    below = edge(raw_clip)
    behind = from_behind(below.reshape(-1, below.shape[-1]), "space", 1).reshape(below.shape)
    fresh, fresh_rows = pool(raw_clip, behind, pool_weight, head_size)
    for d in range(2, half, 2):
        row = d // 2 * tokens
        both = jnp.concatenate([kept[d // 2], near_in[row : row + tokens]], axis=0)
        both = exchange(both, "slot", d)
        sources[d], sources[d + 1] = both[:tokens], both[tokens:]
    order = (None,) + tuple(range(slots))
    bias = mask(place, after(valid_columns, fresh_rows), columns, tokens, order)
    far = exchange(after(near, bias), "space", 1)
    inside = [(i, i + 1) for i in range(0, slots, 2)]
    onward = [(i, i + 1) for i in range(1, slots - 1, 2)]
    inside = lax.ppermute(after(resident, near_in), "slot", inside)
    onward = lax.ppermute(after(resident, *sources.values(), bias), "slot", onward)
    call = partial(
        attend,
        bias,
        sources=[fresh_rows] + [sources[d] for d in range(slots)],
        head_size=head_size,
    )
    parts = []
    for k, e in enumerate(evens):
        rows = slice(k * query_rows, (k + 1) * query_rows)
        (part,) = call(queries=far[rows], travels=True)
        core_part = exchange(part, "space", 1)
        value, level = call(queries=near[rows], travels=False)
        part = merge(value, level, [(core_part, 0)], head_size, True)
        parts.append((exchange(part, "space", e), 0))
        sent_part = part
    (part,) = call(queries=after(far[len(evens) * query_rows :], sent_part), travels=True)
    parts.append((exchange(part, "space", 1), 0))
    value, level = call(queries=own_queries, travels=False, weight=4)
    mixed = merge(value, level, parts, head_size, False)

    blocks = gather(mixed, slots, (inside, onward))
    aged_memory = jnp.where(slot_index % 2 == 1, inside, onward).reshape(old_memory.shape)
    early_weight, late_weight = arrange(place, out_weight, slots)
    total, aged_memory = project_early(early_weight, [blocks[d] for d in range(half)], aged_memory)
    attended = project_late(late_weight, [blocks[d] for d in range(half, slots)], total)
    return (attended, fresh, aged_memory)


def solution(mesh):
    return jax.shard_map(
        local,
        mesh=mesh,
        in_specs=(
            P("space", None),
            P(None, "space", None, "slot"),
            P(None, "slot"),
            P("slot", None, "space", None, None),
            P(),
            P(),
        ),
        out_specs=(
            P("space", None),
            P(None, "space", None, "slot"),
            P("slot", None, "space", None, None),
        ),
        check_vma=False,
    )
```
